256 devices in a mesh: grp: 4 (over x_hi, core), tile: 64 (over z, x_lo, y).
Axes of the slice: x: 4 (x_hi: 2, x_lo: 2; x = x_hi * 2 + x_lo), y: 4, z: 8, core: 2. Of those that a mesh axis runs over, the one named last changes fastest.
Arguments:
- sky: float32 [32, 8192], P(None, 'tile'), may hold values from -6 to 6
- psf_basis: bfloat16 [4, 5, 41, 41], P('grp'), may hold values from -0.15625 to 0.15625
- item_tile: int32 [768], P(('grp', 'tile')), may hold values from 0 to 63, as said below
- warp_corner: int32 [768, 32, 128], P(('grp', 'tile')), may hold values from 0 to 5454, as said below
- warp_weight: bfloat16 [768, 4, 32, 128], P(('grp', 'tile')), may hold values from 0 to 0.5
- psf_coeff: bfloat16 [768, 32, 5, 128], P(('grp', 'tile')), may hold values from -3 to 3
- observed: bfloat16 [768, 32, 128], P(('grp', 'tile')), may hold values from -6 to 6
- inv_var: bfloat16 [768, 32, 128], P(('grp', 'tile')), may hold values from 0.25 to 2
Outputs:
- new_sky: float32 [32, 8192], P(None, 'tile')
The draws below stay inside these ranges and needn't reach their ends.
Inputs may be any that keep to these rules, and one draw needn't show every extreme that they name: `item_tile`: the footprints of the device at index d of tile are its block of 3 consecutive entries; each names a tile of d - 1 to d + 1, the first of every block d itself. `warp_corner`: each value at pixel (r, c) is q * 176 + p with q at most 30, q within 3 of r, and p at most 174.
All inputs are finite; a program needn't handle non-finite values.
Results may differ from the reference program's by a relative error of at most 0.0003.
Values sent between devices are 32-bit elements; how exact they have to be, the bound alone decides.
A program may use at most 128 MiB of HBM per device.

```python
import math
import jax
import jax.numpy as jnp
from jax import lax

ROWS = 32
TILE_COLS = 128
MARGIN = 24
TAPS = 41
NPSF = 5
ITEMS_DEV = 3
ITEMS = 768
SKY_COLS = 8192
GROUPS = 4


def draw_item_tile(key, part):
    key = jax.random.fold_in(key, 11)
    tile_total = SKY_COLS // TILE_COLS
    number = jnp.arange(ITEMS, dtype=jnp.int32)
    owner = number // ITEMS_DEV % tile_total
    moved = jax.random.randint(key, (ITEMS,), -1, 2, dtype=jnp.int32)
    moved = jnp.where(number % ITEMS_DEV == 0, 0, moved)
    return jnp.clip(owner + moved, 0, tile_total - 1).astype(jnp.int32)


def draw_warp_corner(key, part):
    key = jax.random.fold_in(key, 23)
    extent = TILE_COLS + 2 * MARGIN
    row_key, col_key = jax.random.split(key)
    grid_shape = (ITEMS, ROWS, TILE_COLS)
    pixel_row = lax.broadcasted_iota(jnp.int32, grid_shape, 1)
    pixel_col = lax.broadcasted_iota(jnp.int32, grid_shape, 2)
    row_step = jax.random.randint(row_key, grid_shape, -3, 4, dtype=jnp.int32)
    col_step = jax.random.randint(col_key, grid_shape, -MARGIN, MARGIN + 1, dtype=jnp.int32)
    corner_row = jnp.clip(pixel_row + row_step, 0, ROWS - 2)
    corner_col = jnp.clip(pixel_col + MARGIN + col_step, 0, extent - 2)
    corner = corner_row * extent + corner_col
    first_pixel = (pixel_row == 0) & (pixel_col == 0)
    last_pixel = (pixel_row == ROWS - 1) & (pixel_col == TILE_COLS - 1)
    corner = jnp.where(first_pixel, 0, corner)
    corner = jnp.where(last_pixel, (ROWS - 1) * extent - 2, corner)
    return corner.astype(jnp.int32)


def shard_levels(rng, shape, cuts, least, top_value):
    def one(dim, parts):
        steps = jax.random.uniform(jax.random.fold_in(jax.random.fold_in(rng, 6), dim), (parts,), jnp.float32, least / len(cuts), top_value / len(cuts))
        return jnp.repeat(jnp.exp(steps), shape[dim] // parts).reshape((-1,) + (1,) * (len(shape) - dim - 1))

    factor_of = one(*cuts[0])
    for cut in cuts[1:]:
        factor_of = factor_of * one(*cut)
    return factor_of


def gaussian(rng, dims, scale, most, cuts=(), held_as=jnp.bfloat16):
    entries = jax.random.normal(rng, dims, jnp.float32) * scale
    if len(cuts) > 0:
        entries = shard_levels(rng, dims, cuts, -0.22, 0.18) * entries
    return jnp.clip(entries, min=-most, max=most).astype(held_as)


def setup_inputs(seed: int = 0) -> dict:
    key_list = jax.random.split(jax.random.key(seed), 9)
    return {
        "sky": gaussian(key_list[0], (ROWS, SKY_COLS), 1.0, 6.0, ((1, 64),), jnp.float32),
        "psf_basis": gaussian(key_list[1], (GROUPS, NPSF, TAPS, TAPS), (TAPS * TAPS) ** -0.5, 0.15625, ((0, 4),)),
        "item_tile": draw_item_tile(jax.random.fold_in(key_list[8], 71), 0),
        "warp_corner": draw_warp_corner(jax.random.fold_in(key_list[8], 71), 0),
        "warp_weight": jnp.clip(0.5 * jax.random.uniform(key_list[4], (ITEMS, 4, ROWS, TILE_COLS), jnp.float32) ** shard_levels(key_list[4], (ITEMS, 4, ROWS, TILE_COLS), ((0, 256),), -0.2, 0.2), 0.0, 0.5).astype(jnp.bfloat16),
        "psf_coeff": gaussian(key_list[5], (ITEMS, ROWS, NPSF, TILE_COLS), 0.5, 3.0, ((0, 256),)),
        "observed": gaussian(key_list[6], (ITEMS, ROWS, TILE_COLS), 1.0, 6.0, ((0, 256),)),
        "inv_var": jnp.clip(jnp.exp(math.log(2.0) - 2.0794415 * jax.random.uniform(key_list[7], (ITEMS, ROWS, TILE_COLS), jnp.float32) ** shard_levels(key_list[7], (ITEMS, ROWS, TILE_COLS), ((0, 256),), -0.2, 0.2)), 0.25, 2.0).astype(jnp.bfloat16),
    }


step_size = 0.25


def psf_table(eigen_psf):
    tap_count = eigen_psf.shape[-1]
    middle = tap_count // 2
    target = jnp.arange(TILE_COLS).astype(jnp.int32)[:, None]
    source = jnp.arange(TILE_COLS).astype(jnp.int32)[None, :]
    spread = target - source + middle
    inside = (spread >= 0) & (spread < tap_count)
    clipped = jnp.clip(spread, 0, tap_count - 1).astype(jnp.int32)
    tap_table = eigen_psf[:, :, clipped]
    return jnp.where(inside[None, None], tap_table, jnp.zeros_like(tap_table))


def reference(sky, psf_basis, item_tile, warp_corner, warp_weight, psf_coeff, observed, inv_var):
    tap_count = psf_basis.shape[-1]
    psf_count = psf_basis.shape[1]
    middle = tap_count // 2
    region_width = SKY_COLS + 2 * MARGIN
    extent = TILE_COLS + 2 * MARGIN
    widened = jnp.pad(sky, ((0, 0), (MARGIN, MARGIN))).reshape(-1)
    tables = jax.vmap(psf_table)(psf_basis)
    forward_all = tables.transpose(0, 2, 3, 1, 4).reshape(GROUPS, tap_count * TILE_COLS, psf_count * TILE_COLS).astype(jnp.float32)
    adjoint_all = tables.transpose(0, 2, 1, 4, 3).reshape(GROUPS, tap_count * psf_count * TILE_COLS, TILE_COLS).astype(jnp.float32)
    per_group = ITEMS_DEV * (SKY_COLS // TILE_COLS)

    def one_item(total, inputs):
        number, tile_id, corner, weight, coeff, seen, precision_map = inputs
        group_id = (number // per_group).astype(jnp.int32)
        forward_matrix = forward_all[group_id]
        adjoint_matrix = adjoint_all[group_id]
        corner_row = corner // extent
        corner_col = corner % extent
        position = (corner_row * region_width + tile_id * TILE_COLS + corner_col).astype(jnp.int32)
        stencil = jnp.stack([position, position + 1, position + region_width, position + region_width + 1], axis=0)
        weight_f = weight.astype(jnp.float32)
        warped = jnp.sum(weight_f * widened[stencil], axis=0)
        lifted = jnp.pad(warped, ((middle, middle), (0, 0)))
        stacked = jnp.stack([lifted[offset:offset + ROWS] for offset in range(tap_count)], axis=1).reshape(ROWS, tap_count * TILE_COLS)
        blurred = jnp.dot(stacked, forward_matrix, precision=lax.Precision.HIGHEST).reshape(ROWS, psf_count, TILE_COLS)
        coeff_f = coeff.astype(jnp.float32)
        predicted = jnp.sum(blurred * coeff_f, axis=1)
        misfit = precision_map.astype(jnp.float32) * (predicted - seen.astype(jnp.float32))
        weighted = coeff_f * misfit[:, None, :]
        lowered = jnp.pad(weighted, ((middle, middle), (0, 0), (0, 0)))
        stacked_back = jnp.stack([lowered[2 * middle - offset:2 * middle - offset + ROWS] for offset in range(tap_count)], axis=1).reshape(ROWS, tap_count * psf_count * TILE_COLS)
        backward = jnp.dot(stacked_back, adjoint_matrix, precision=lax.Precision.HIGHEST)
        spread = weight_f * backward[None]
        total = total.at[stencil.reshape(-1)].add(spread.reshape(-1))
        return total, None

    numbers = jnp.arange(ITEMS).astype(jnp.int32)
    start = jnp.zeros((ROWS * region_width,), jnp.float32)
    total, _ = lax.scan(one_item, start, (numbers, item_tile, warp_corner, warp_weight, psf_coeff, observed, inv_var))
    gradient = total.reshape(ROWS, region_width)[:, MARGIN:MARGIN + SKY_COLS]
    return sky - step_size * gradient
```

```python
import functools

import jax
import jax.numpy as jnp
from jax import lax
from jax.experimental import pallas as pl
from jax.experimental.pallas import tpu as pltpu
from jax.sharding import PartitionSpec as P

F32, BF16, I32 = jnp.float32, jnp.bfloat16, jnp.int32
ROWS, COLS, MARGIN, TAPS, NPSF, ITEMS = 32, 128, 24, 41, 5, 3
EXTENT = COLS + 2 * MARGIN
HALF = TAPS // 2
WIDE = ITEMS * COLS
DEPTH = TAPS * ROWS
GROUPS_OF_4 = (TAPS + 3) // 4
PAD = 8
STEP = 0.25
OFFSETS = (-2, -1, 1, 2)
SLOT = {-2: 0, -1: 1, 0: 2, 1: 3, 2: 4}


def split(value):
    high = value.astype(BF16)
    return high, (value - high.astype(F32)).astype(BF16)


def nt_dot(a, b):
    return lax.dot_general(a, b, (((1,), (1,)), ((), ())), preferred_element_type=F32)


def prepare(psf, corner, coeff, tap_rows, tap_cols, blur_left, blur_right, coeff_wide, coeff_f, hot):
    tap_rows[...] = jnp.zeros_like(tap_rows)
    for k in range(NPSF):
        tap_rows[k, pl.ds(0, TAPS), pl.ds(0, TAPS)] = psf[0, k].astype(F32)
    for k in range(NPSF):
        tap_cols[k] = pltpu.roll(tap_rows[k], 4, 0).T
    lane_group = lax.broadcasted_iota(I32, (8, COLS), 1) // ROWS

    def tap_tile(j, _):
        whole = []
        for k in range(NPSF):
            for r0 in range(0, ROWS, 8):
                tile = jnp.zeros((8, COLS), F32)
                for part in range(4):
                    row = jnp.broadcast_to(tap_cols[k, pl.ds(4 * j + part, 1), :], (8, COLS))
                    turned = pltpu.roll(row, (r0 + ROWS * part - HALF - 4) % COLS, 1, stride=1, stride_axis=0)
                    tile = turned if part == 0 else jnp.where(lane_group == part, turned, tile)
                whole.append(tile)
        whole = jnp.concatenate(whole, axis=0)
        at = pl.multiple_of(j * COLS, COLS)
        blur_left[:, pl.ds(at, COLS)] = whole.astype(BF16)
        blur_right[pl.ds(at, COLS), :] = whole.T.astype(BF16)
        return 0

    lax.fori_loop(0, GROUPS_OF_4, tap_tile, 0)
    for n in range(ITEMS):
        coeff_wide[:, pl.ds(0, NPSF), :] = coeff[n].astype(F32)
        for k in range(NPSF):
            coeff_f[k, :, pl.ds(n * COLS, COLS)] = coeff_wide[:, k, :]
    column = lax.broadcasted_iota(I32, (EXTENT, COLS), 0)

    def hot_rows(step, _):
        n, pair = step // 8, lax.rem(step, 8)
        for u in range(4):
            r = pair * 4 + u
            at = corner[n, pl.ds(r, 1), :]
            start = at - ((at * 23832) >> 22) * EXTENT
            hot[n, pair // 2, :, pl.ds(pl.multiple_of((lax.rem(pair, 2) * 4 + u) * COLS, COLS), COLS)] = jnp.where(
                column == start, 1.0, 0.0
            ).astype(BF16)
        return 0

    lax.fori_loop(0, ITEMS * 8, hot_rows, 0)


def warp(me, tiles, corner, weight, region, sides, warped):
    lane = lax.broadcasted_iota(I32, (ROWS, COLS), 1)
    for t in range(3):
        left = region[t, pl.ds(PAD, ROWS), :]
        right = region[t + 2, pl.ds(PAD, ROWS), :]
        if t < 2:
            left = jnp.where(me - 2 + t >= 0, left, 0.0)
        if t > 0:
            right = jnp.where(me + t <= lax.axis_size("tile") - 1, right, 0.0)
        sides[t, pl.ds(PAD, ROWS), :] = jnp.where(lane >= COLS // 2, left, right)

    def one(step, _):
        n, block = step // 4, lax.rem(step, 4)
        r0 = pl.multiple_of(block * 8, 8)
        t = jnp.clip(tiles[n] - (me - 1), 0, 2)
        at = corner[n, pl.ds(r0, 8), :]
        q = (at * 23832) >> 22
        p = at - q * EXTENT
        rel = q - (lax.broadcasted_iota(I32, (8, COLS), 0) + r0) + 3
        total = jnp.zeros((8, COLS), F32)
        for dp in range(2):
            index = (p + (dp + COLS - MARGIN)) & (COLS - 1)
            middle = (p + dp >= MARGIN) & (p + dp < MARGIN + COLS)
            upper = jnp.zeros((8, COLS), F32)
            lower = jnp.zeros((8, COLS), F32)
            for o in range(8):
                rows = pl.ds(r0 + (PAD - 3 + o), 8)
                inside = jnp.take_along_axis(region[t + 1, rows, :], index, axis=1)
                beside = jnp.take_along_axis(sides[t, rows, :], index, axis=1)
                found = jnp.where(middle, inside, beside)
                if o < 7:
                    upper = jnp.where(rel == o, found, upper)
                if o > 0:
                    lower = jnp.where(rel == o - 1, found, lower)
            total += weight[n, dp, pl.ds(r0, 8), :].astype(F32) * upper
            total += weight[n, 2 + dp, pl.ds(r0, 8), :].astype(F32) * lower
        warped[n, pl.ds(r0, 8), :] = total
        return 0

    lax.fori_loop(0, ITEMS * 4, one, 0)


def blur_and_back(obs, ivar, warped, lifted, blur_left, blur_right, coeff_f, misfit_parts, spread, backward):
    lane = lax.broadcasted_iota(I32, (ROWS, COLS), 1)

    def lift(b, _):
        shift = lax.rem(HALF - b + COLS, COLS)
        source = lane + (b - HALF)
        inside = (source >= 0) & (source < COLS)
        at = pl.multiple_of(b * ROWS, ROWS)
        for n in range(ITEMS):
            value = jnp.where(inside, pltpu.roll(warped[n], shift, 1), 0.0)
            high, low = split(value)
            lifted[pl.ds(at, ROWS), pl.ds(n * COLS, COLS)] = high
            lifted[pl.ds(at, ROWS), pl.ds(WIDE + n * COLS, COLS)] = low
        return 0

    lax.fori_loop(0, TAPS, lift, 0)
    both = jnp.dot(blur_left[:, pl.ds(0, DEPTH)], lifted[...], preferred_element_type=F32)
    blurred = both[:, :WIDE] + both[:, WIDE:]
    predicted = jnp.zeros((ROWS, WIDE), F32)
    for k in range(NPSF):
        predicted += coeff_f[k] * blurred[k * ROWS : (k + 1) * ROWS]
    misfit = []
    for n in range(ITEMS):
        misfit.append(
            ivar[n].astype(F32) * (predicted[:, n * COLS : (n + 1) * COLS] - obs[n].astype(F32))
        )
    misfit = jnp.concatenate(misfit, axis=1)
    for k in range(NPSF):
        high, low = split(coeff_f[k] * misfit)
        misfit_parts[pl.ds(k * ROWS, ROWS), pl.ds(0, WIDE)] = high
        misfit_parts[pl.ds(k * ROWS, ROWS), pl.ds(WIDE, WIDE)] = low
    spread[...] = jnp.dot(blur_right[pl.ds(0, DEPTH), :], misfit_parts[...], preferred_element_type=F32)

    def lower(b, sums):
        shift = lax.rem(b - HALF + COLS, COLS)
        source = lane - (b - HALF)
        inside = (source >= 0) & (source < COLS)
        at = pl.multiple_of(b * ROWS, ROWS)
        out = []
        for n in range(ITEMS):
            value = spread[pl.ds(at, ROWS), pl.ds(n * COLS, COLS)]
            value += spread[pl.ds(at, ROWS), pl.ds(WIDE + n * COLS, COLS)]
            out.append(sums[n] + jnp.where(inside, pltpu.roll(value, shift, 1), 0.0))
        return tuple(out)

    zero = jnp.zeros((ROWS, COLS), F32)
    sums = lax.fori_loop(0, TAPS, lower, (zero,) * ITEMS)
    for n in range(ITEMS):
        backward[n] = sums[n]


def scatter(me, tiles, corner, weight, backward, hot, window_grad, gradient):
    window_grad[...] = jnp.zeros_like(window_grad)

    def one(step, _):
        n, block = step // 4, lax.rem(step, 4)
        r0 = pl.multiple_of(block * 8, 8)
        q = ((corner[n, pl.ds(r0, 8), :] * 23832) >> 22) - (r0 - 4)
        parts = []
        for j in range(4):
            value = weight[n, j, pl.ds(r0, 8), :].astype(F32) * backward[n, pl.ds(r0, 8), :]
            high = value.astype(BF16).astype(F32)
            parts.append((high, value - high))
        target = lax.broadcasted_iota(I32, (16, COLS), 0)
        columns = []
        for u in range(8):
            row = jnp.broadcast_to(q[u : u + 1], (16, COLS))
            first, second = target == row, target == row + 1
            stack = []
            for dp in range(2):
                for half in range(2):
                    one_up = jnp.broadcast_to(parts[dp][half][u : u + 1], (16, COLS))
                    one_low = jnp.broadcast_to(parts[2 + dp][half][u : u + 1], (16, COLS))
                    stack.append(jnp.where(first, one_up, jnp.where(second, one_low, 0.0)).astype(BF16))
            columns.append(jnp.concatenate(stack, axis=0))
        values = jnp.concatenate(columns, axis=1)
        found = nt_dot(values, hot[n, block])
        for dp in range(2):
            part = found[dp * 32 : dp * 32 + 16] + found[dp * 32 + 16 : dp * 32 + 32]
            window_grad[n, dp, pl.ds(r0, 16), pl.ds(0, EXTENT)] += part
        return 0

    lax.fori_loop(0, ITEMS * 4, one, 0)
    lane = lax.broadcasted_iota(I32, (ROWS, COLS), 1)
    left_lanes = lane >= COLS // 2
    totals = [jnp.zeros((ROWS, COLS), F32) for _ in range(5)]
    for n in range(ITEMS):
        t = jnp.clip(tiles[n] - (me - 1), 0, 2)
        whole = pltpu.roll(window_grad[n, 0, pl.ds(4, ROWS), :], COLS - MARGIN, 1)
        whole += pltpu.roll(window_grad[n, 1, pl.ds(4, ROWS), :], COLS - MARGIN + 1, 1)
        beside, inside = whole[:, :COLS], whole[:, COLS:]
        left = jnp.where(left_lanes, beside, 0.0)
        right = jnp.where(left_lanes, 0.0, beside)
        for s in range(5):
            if n == 0 and s not in (1, 2, 3):
                continue
            if s - 1 in (0, 1, 2):
                totals[s] += jnp.where(t == s - 1, inside, 0.0)
            if s in (0, 1, 2):
                totals[s] += jnp.where(t == s, left, 0.0)
            if s - 2 in (0, 1, 2):
                totals[s] += jnp.where(t == s - 2, right, 0.0)
    for s in range(5):
        gradient[s] = totals[s]


def kernel(tiles, sky, psf, corner, weight, coeff, obs, ivar, out,
           region, arrived, groups, sides, tap_rows, tap_cols, blur_left, blur_right, coeff_wide, coeff_f,
           hot, warped, lifted, misfit_parts, spread, backward, window_grad, gradient,
           near_send, near_recv, back_send, back_recv, grp_send, grp_recv):
    me, grp = lax.axis_index("tile"), lax.axis_index("grp")
    count, group_count = lax.axis_size("tile"), lax.axis_size("grp")

    def tile_at(offset):
        return lax.rem(me + offset + count, count)

    barrier = pltpu.get_barrier_semaphore()
    for offset in OFFSETS:
        pl.semaphore_signal(barrier, inc=1, device_id=(grp, tile_at(offset)), device_id_type=pl.DeviceIdType.MESH)
    for step in range(1, group_count):
        pl.semaphore_signal(
            barrier, inc=1, device_id=(lax.rem(grp + step, group_count), me), device_id_type=pl.DeviceIdType.MESH
        )
    pl.semaphore_wait(barrier, 4 + group_count - 1)

    near = []
    for number, offset in enumerate(OFFSETS):
        copy = pltpu.make_async_remote_copy(
            src_ref=sky,
            dst_ref=region.at[SLOT[-offset], pl.ds(PAD, ROWS), :],
            send_sem=near_send.at[number],
            recv_sem=near_recv.at[number],
            device_id=(grp, tile_at(offset)),
            device_id_type=pl.DeviceIdType.MESH,
        )
        copy.start()
        near.append(copy)
    region[2, pl.ds(PAD, ROWS), :] = sky[...]
    prepare(psf, corner, coeff, tap_rows, tap_cols, blur_left, blur_right, coeff_wide, coeff_f, hot)
    for copy in near:
        copy.wait()
    warp(me, tiles, corner, weight, region, sides, warped)
    blur_and_back(obs, ivar, warped, lifted, blur_left, blur_right, coeff_f, misfit_parts, spread, backward)
    scatter(me, tiles, corner, weight, backward, hot, window_grad, gradient)

    back = []
    for number, offset in enumerate(OFFSETS):
        copy = pltpu.make_async_remote_copy(
            src_ref=gradient.at[SLOT[offset]],
            dst_ref=arrived.at[number],
            send_sem=back_send.at[number],
            recv_sem=back_recv.at[number],
            device_id=(grp, tile_at(offset)),
            device_id_type=pl.DeviceIdType.MESH,
        )
        copy.start()
        back.append(copy)
    owned = gradient[2]
    for number, offset in enumerate(OFFSETS):
        back[number].wait()
        valid = (me - offset >= 0) & (me - offset <= count - 1)
        owned += jnp.where(valid, arrived[number], 0.0)
    groups[grp] = owned
    sums = []
    for step in range(1, group_count):
        copy = pltpu.make_async_remote_copy(
            src_ref=groups.at[grp],
            dst_ref=groups.at[grp],
            send_sem=grp_send.at[step - 1],
            recv_sem=grp_recv.at[step - 1],
            device_id=(lax.rem(grp + step, group_count), me),
            device_id_type=pl.DeviceIdType.MESH,
        )
        copy.start()
        sums.append(copy)
    for copy in sums:
        copy.wait()
    total = groups[0]
    for g in range(1, group_count):
        total += groups[g]
    out[...] = sky[...] - STEP * total


def per_device(sky, psf_basis, item_tile, warp_corner, warp_weight, psf_coeff, observed, inv_var):
    group_count = lax.axis_size("grp")
    vmem = pl.BlockSpec(memory_space=pltpu.VMEM)
    dma = pltpu.SemaphoreType.DMA
    return pl.pallas_call(
        kernel,
        out_shape=jax.ShapeDtypeStruct((ROWS, COLS), F32),
        in_specs=[pl.BlockSpec(memory_space=pltpu.SMEM)] + [vmem] * 7,
        out_specs=vmem,
        scratch_shapes=[
            pltpu.VMEM((5, ROWS + 2 * PAD, COLS), F32),
            pltpu.VMEM((4, ROWS, COLS), F32),
            pltpu.VMEM((group_count, ROWS, COLS), F32),
            pltpu.VMEM((3, ROWS + 2 * PAD, COLS), F32),
            pltpu.VMEM((NPSF, COLS, COLS), F32),
            pltpu.VMEM((NPSF, COLS, COLS), F32),
            pltpu.VMEM((NPSF * ROWS, GROUPS_OF_4 * COLS), BF16),
            pltpu.VMEM((GROUPS_OF_4 * COLS, NPSF * ROWS), BF16),
            pltpu.VMEM((ROWS, 8, COLS), F32),
            pltpu.VMEM((NPSF, ROWS, WIDE), F32),
            pltpu.VMEM((ITEMS, 4, EXTENT, 8 * COLS), BF16),
            pltpu.VMEM((ITEMS, ROWS, COLS), F32),
            pltpu.VMEM((DEPTH, 2 * WIDE), BF16),
            pltpu.VMEM((NPSF * ROWS, 2 * WIDE), BF16),
            pltpu.VMEM((DEPTH, 2 * WIDE), F32),
            pltpu.VMEM((ITEMS, ROWS, COLS), F32),
            pltpu.VMEM((ITEMS, 2, ROWS + 8, 2 * COLS), F32),
            pltpu.VMEM((5, ROWS, COLS), F32),
            dma((4,)), dma((4,)), dma((4,)), dma((4,)), dma((group_count - 1,)), dma((group_count - 1,)),
        ],
        compiler_params=pltpu.CompilerParams(
            collective_id=0, has_side_effects=True, vmem_limit_bytes=48 * 2**20
        ),
    )(item_tile, sky, psf_basis, warp_corner, warp_weight, psf_coeff, observed, inv_var)


def solution(mesh):
    return jax.shard_map(
        per_device,
        mesh=mesh,
        in_specs=(
            P(None, "tile"),
            P("grp", None, None, None),
            P(("grp", "tile")),
            P(("grp", "tile"), None, None),
            P(("grp", "tile"), None, None, None),
            P(("grp", "tile"), None, None, None),
            P(("grp", "tile"), None, None),
            P(("grp", "tile"), None, None),
        ),
        out_specs=P(None, "tile"),
        check_vma=False,
    )
```

```python
import functools

import jax
import jax.numpy as jnp
from jax import lax
from jax.experimental import pallas as pl
from jax.experimental.pallas import tpu as pltpu
from jax.sharding import PartitionSpec as P

F32, BF16, I32 = jnp.float32, jnp.bfloat16, jnp.int32
ROWS, COLS, MARGIN, TAPS, NPSF, ITEMS = 32, 128, 24, 41, 5, 3
EXTENT = COLS + 2 * MARGIN
HALF = TAPS // 2
WIDE = ITEMS * COLS
DEPTH = TAPS * ROWS
GROUPS_OF_4 = (TAPS + 3) // 4
PAD = 8
STEP = 0.25
OFFSETS = (-2, -1, 1, 2)
SLOT = {-2: 0, -1: 1, 0: 2, 1: 3, 2: 4}


def split(value):
    high = value.astype(BF16)
    return high, (value - high.astype(F32)).astype(BF16)


def nt_dot(a, b):
    return lax.dot_general(a, b, (((1,), (1,)), ((), ())), preferred_element_type=F32)


def prepare_hot(corner, hot):
    column = lax.broadcasted_iota(I32, (EXTENT, COLS), 0)

    def hot_rows(step, _):
        n, block = step // 4, lax.rem(step, 4)
        at = corner[n, pl.ds(pl.multiple_of(block * 8, 8), 8), :]
        start = at - ((at * 23832) >> 22) * EXTENT
        for u in range(8):
            row = jnp.broadcast_to(start[u : u + 1], (EXTENT, COLS))
            hot[n, block, :, pl.ds(u * COLS, COLS)] = jnp.where(column == row, 1.0, 0.0).astype(BF16)
        return 0

    lax.fori_loop(0, ITEMS * 4, hot_rows, 0)


def prepare_taps(psf, tap_rows, tap_cols, blur_left, blur_right):
    tap_rows[...] = jnp.zeros_like(tap_rows)
    for k in range(NPSF):
        tap_rows[k, pl.ds(0, TAPS), pl.ds(0, TAPS)] = psf[0, k].astype(F32)
    for k in range(NPSF):
        tap_cols[k] = pltpu.roll(tap_rows[k], 4, 0).T
    lane_group = lax.broadcasted_iota(I32, (8, COLS), 1) // ROWS
    for j in range(GROUPS_OF_4):
        whole = []
        for k in range(NPSF):
            for r0 in range(0, ROWS, 8):
                tile = jnp.zeros((8, COLS), F32)
                for part in range(4):
                    row = jnp.broadcast_to(tap_cols[k, pl.ds(4 * j + part, 1), :], (8, COLS))
                    turned = pltpu.roll(row, (r0 + ROWS * part - HALF - 4) % COLS, 1, stride=1, stride_axis=0)
                    tile = turned if part == 0 else jnp.where(lane_group == part, turned, tile)
                whole.append(tile)
        whole = jnp.concatenate(whole, axis=0)
        blur_left[:, pl.ds(j * COLS, COLS)] = whole.astype(BF16)
        blur_right[pl.ds(j * COLS, COLS), :] = whole.T.astype(BF16)


def warp(me, count, tiles, corner, weight, region, sides, warped):
    lane = lax.broadcasted_iota(I32, (ROWS, COLS), 1)
    for t in range(3):
        left = region[t, pl.ds(PAD, ROWS), :]
        right = region[t + 2, pl.ds(PAD, ROWS), :]
        if t < 2:
            left = jnp.where(me - 2 + t >= 0, left, 0.0)
        if t > 0:
            right = jnp.where(me + t <= count - 1, right, 0.0)
        sides[t, pl.ds(PAD, ROWS), :] = jnp.where(lane >= COLS // 2, left, right)
    for n in range(ITEMS):
        t = jnp.clip(tiles[n] - (me - 1), 0, 2)
        for r0 in range(0, ROWS, 8):
            at = corner[n, pl.ds(r0, 8), :]
            q = (at * 23832) >> 22
            p = at - q * EXTENT
            rel = q - (lax.broadcasted_iota(I32, (8, COLS), 0) + r0) + 3
            total = jnp.zeros((8, COLS), F32)
            for dp in range(2):
                index = (p + (dp + COLS - MARGIN)) & (COLS - 1)
                middle = (p + dp >= MARGIN) & (p + dp < MARGIN + COLS)
                upper = jnp.zeros((8, COLS), F32)
                lower = jnp.zeros((8, COLS), F32)
                for o in range(8):
                    rows = pl.ds(r0 + (PAD - 3 + o), 8)
                    inside = jnp.take_along_axis(region[t + 1, rows, :], index, axis=1)
                    beside = jnp.take_along_axis(sides[t, rows, :], index, axis=1)
                    found = jnp.where(middle, inside, beside)
                    if o < 7:
                        upper = jnp.where(rel == o, found, upper)
                    if o > 0:
                        lower = jnp.where(rel == o - 1, found, lower)
                total += weight[n, dp, pl.ds(r0, 8), :].astype(F32) * upper
                total += weight[n, 2 + dp, pl.ds(r0, 8), :].astype(F32) * lower
            warped[n, pl.ds(r0, 8), :] = total


def blur(coeff, obs, ivar, warped, lifted, blur_left, misfit_parts):
    lane = lax.broadcasted_iota(I32, (ROWS, COLS), 1)
    for b in range(TAPS):
        source = lane + (b - HALF)
        inside = (source >= 0) & (source < COLS)
        for n in range(ITEMS):
            value = warped[n]
            if b != HALF:
                value = jnp.where(inside, pltpu.roll(value, (HALF - b) % COLS, 1), 0.0)
            high, low = split(value)
            lifted[pl.ds(b * ROWS, ROWS), pl.ds(n * COLS, COLS)] = high
            lifted[pl.ds(b * ROWS, ROWS), pl.ds(WIDE + n * COLS, COLS)] = low
    both = jnp.dot(blur_left[:, pl.ds(0, DEPTH)], lifted[...], preferred_element_type=F32)
    blurred = both[:, :WIDE] + both[:, WIDE:]
    for n in range(ITEMS):
        predicted = jnp.zeros((ROWS, COLS), F32)
        for k in range(NPSF):
            predicted += coeff[n, k].astype(F32) * blurred[k * ROWS : (k + 1) * ROWS, n * COLS : (n + 1) * COLS]
        misfit = ivar[n].astype(F32) * (predicted - obs[n].astype(F32))
        for k in range(NPSF):
            high, low = split(coeff[n, k].astype(F32) * misfit)
            misfit_parts[pl.ds(k * ROWS, ROWS), pl.ds(n * COLS, COLS)] = high
            misfit_parts[pl.ds(k * ROWS, ROWS), pl.ds(WIDE + n * COLS, COLS)] = low


def back(blur_right, misfit_parts, spread, backward):
    lane = lax.broadcasted_iota(I32, (ROWS, COLS), 1)
    spread[...] = jnp.dot(blur_right[pl.ds(0, DEPTH), :], misfit_parts[...], preferred_element_type=F32)
    for n in range(ITEMS):
        total = jnp.zeros((ROWS, COLS), F32)
        for b in range(TAPS):
            source = lane - (b - HALF)
            inside = (source >= 0) & (source < COLS)
            value = spread[pl.ds(b * ROWS, ROWS), pl.ds(n * COLS, COLS)]
            value += spread[pl.ds(b * ROWS, ROWS), pl.ds(WIDE + n * COLS, COLS)]
            if b != HALF:
                value = jnp.where(inside, pltpu.roll(value, (b - HALF) % COLS, 1), 0.0)
            total += value
        backward[n] = total


def scatter(corner, weight, backward, hot, parts, window_grad):
    window_grad[...] = jnp.zeros_like(window_grad)
    target = lax.broadcasted_iota(I32, (16, COLS), 0)
    for n in range(ITEMS):
        for j in range(4):
            value = weight[n, j].astype(F32) * backward[n]
            high = value.astype(BF16).astype(F32)
            parts[n, j, 0] = high
            parts[n, j, 1] = value - high
        for block in range(4):
            r0 = block * 8
            q = ((corner[n, pl.ds(r0, 8), :] * 23832) >> 22) - (r0 - 4)
            columns = []
            for u in range(8):
                row = jnp.broadcast_to(q[u : u + 1], (16, COLS))
                first, second = target == row, target == row + 1
                stack = []
                for dp in range(2):
                    for half in range(2):
                        one_up = jnp.broadcast_to(parts[n, dp, half, pl.ds(r0 + u, 1), :], (16, COLS))
                        one_low = jnp.broadcast_to(parts[n, 2 + dp, half, pl.ds(r0 + u, 1), :], (16, COLS))
                        stack.append(jnp.where(first, one_up, jnp.where(second, one_low, 0.0)).astype(BF16))
                columns.append(jnp.concatenate(stack, axis=0))
            values = jnp.concatenate(columns, axis=1)
            found = nt_dot(values, hot[n, block])
            for dp in range(2):
                part = found[dp * 32 : dp * 32 + 16] + found[dp * 32 + 16 : dp * 32 + 32]
                window_grad[n, dp, pl.ds(r0, 16), pl.ds(0, EXTENT)] += part


def gather_tiles(me, tiles, window_grad, gradient):
    lane = lax.broadcasted_iota(I32, (ROWS, COLS), 1)
    left_lanes = lane >= COLS // 2
    totals = [jnp.zeros((ROWS, COLS), F32) for _ in range(5)]
    for n in range(ITEMS):
        t = jnp.clip(tiles[n] - (me - 1), 0, 2)
        whole = pltpu.roll(window_grad[n, 0, pl.ds(4, ROWS), :], COLS - MARGIN, 1)
        whole += pltpu.roll(window_grad[n, 1, pl.ds(4, ROWS), :], COLS - MARGIN + 1, 1)
        beside, inside = whole[:, :COLS], whole[:, COLS:]
        left = jnp.where(left_lanes, beside, 0.0)
        right = jnp.where(left_lanes, 0.0, beside)
        for s in range(5):
            if n == 0 and s not in (1, 2, 3):
                continue
            if s - 1 in (0, 1, 2):
                totals[s] += jnp.where(t == s - 1, inside, 0.0)
            if s in (0, 1, 2):
                totals[s] += jnp.where(t == s, left, 0.0)
            if s - 2 in (0, 1, 2):
                totals[s] += jnp.where(t == s - 2, right, 0.0)
    for s in range(5):
        gradient[s] = totals[s]


def kernel(tiles, sky_hbm, psf, corner_hbm, weight_hbm, coeff_hbm, obs_hbm, ivar_hbm, out,
           corner, weight, coeff, obs, ivar,
           region, arrived, groups, sides, tap_rows, tap_cols, blur_left, blur_right,
           hot, warped, lifted, misfit_parts, spread, backward, parts, window_grad, gradient,
           load, near_send, near_recv, back_send, back_recv, grp_send, grp_recv):
    me, grp = lax.axis_index("tile"), lax.axis_index("grp")
    count, group_count = lax.axis_size("tile"), lax.axis_size("grp")
    mesh_id = pl.DeviceIdType.MESH
    there = {offset: (me + offset >= 0) & (me + offset <= count - 1) for offset in OFFSETS}
    barrier = pltpu.get_barrier_semaphore()
    for offset in OFFSETS:
        @pl.when(there[offset])
        def _():
            pl.semaphore_signal(barrier, inc=1, device_id=(grp, me + offset), device_id_type=mesh_id)
    for step in range(1, group_count):
        other = lax.rem(grp + step, group_count)
        pl.semaphore_signal(barrier, inc=1, device_id=(other, me), device_id_type=mesh_id)
    sky_here = region.at[2, pl.ds(PAD, ROWS), :]
    pairs = ((corner_hbm, corner), (sky_hbm, sky_here), (weight_hbm, weight),
             (coeff_hbm, coeff), (obs_hbm, obs), (ivar_hbm, ivar))
    loads = [pltpu.make_async_copy(a, b, load.at[i]) for i, (a, b) in enumerate(pairs)]
    for copy in loads:
        copy.start()
    loads[0].wait()
    prepare_hot(corner, hot)
    pl.semaphore_wait(barrier, jnp.minimum(me, 2) + jnp.minimum(count - 1 - me, 2) + group_count - 1)

    near = []
    for number, offset in enumerate(OFFSETS):
        near.append(pltpu.make_async_remote_copy(
            src_ref=sky_hbm,
            dst_ref=region.at[SLOT[-offset], pl.ds(PAD, ROWS), :],
            send_sem=near_send.at[number],
            recv_sem=near_recv.at[number],
            device_id=(grp, me + offset),
            device_id_type=mesh_id,
        ))
        pl.when(there[offset])(near[number].start)
    prepare_taps(psf, tap_rows, tap_cols, blur_left, blur_right)
    for copy in loads[1:]:
        copy.wait()
    for number, offset in enumerate(OFFSETS):
        pl.when(there[-offset])(near[number].wait_recv)
    warp(me, count, tiles, corner, weight, region, sides, warped)
    blur(coeff, obs, ivar, warped, lifted, blur_left, misfit_parts)
    back(blur_right, misfit_parts, spread, backward)
    scatter(corner, weight, backward, hot, parts, window_grad)
    gather_tiles(me, tiles, window_grad, gradient)

    home = []
    for number, offset in enumerate(OFFSETS):
        home.append(pltpu.make_async_remote_copy(
            src_ref=gradient.at[SLOT[offset]],
            dst_ref=arrived.at[number],
            send_sem=back_send.at[number],
            recv_sem=back_recv.at[number],
            device_id=(grp, me + offset),
            device_id_type=mesh_id,
        ))
        pl.when(there[offset])(home[number].start)
    owned = gradient[2]
    for number, offset in enumerate(OFFSETS):
        pl.when(there[-offset])(home[number].wait_recv)
        owned += jnp.where(there[-offset], arrived[number], 0.0)
    groups[grp] = owned
    sums = []
    for step in range(1, group_count):
        sums.append(pltpu.make_async_remote_copy(
            src_ref=groups.at[grp],
            dst_ref=groups.at[grp],
            send_sem=grp_send.at[step - 1],
            recv_sem=grp_recv.at[step - 1],
            device_id=(lax.rem(grp + step, group_count), me),
            device_id_type=mesh_id,
        ))
        sums[-1].start()
    for number, offset in enumerate(OFFSETS):
        pl.when(there[offset])(near[number].wait_send)
        pl.when(there[offset])(home[number].wait_send)
    for copy in sums:
        copy.wait()
    total = groups[0]
    for g in range(1, group_count):
        total += groups[g]
    out[...] = region[2, pl.ds(PAD, ROWS), :] - STEP * total


def per_device(sky, psf_basis, item_tile, warp_corner, warp_weight, psf_coeff, observed, inv_var):
    group_count = lax.axis_size("grp")
    vmem = pl.BlockSpec(memory_space=pltpu.VMEM)
    dma = pltpu.SemaphoreType.DMA
    hbm = pl.BlockSpec(memory_space=pltpu.HBM)
    coeff = psf_coeff.transpose(0, 2, 1, 3)
    return pl.pallas_call(
        kernel,
        out_shape=jax.ShapeDtypeStruct((ROWS, COLS), F32),
        in_specs=[pl.BlockSpec(memory_space=pltpu.SMEM), hbm, vmem] + [hbm] * 5,
        out_specs=vmem,
        scratch_shapes=[
            pltpu.VMEM(warp_corner.shape, I32),
            pltpu.VMEM(warp_weight.shape, BF16),
            pltpu.VMEM(coeff.shape, BF16),
            pltpu.VMEM(observed.shape, BF16),
            pltpu.VMEM(inv_var.shape, BF16),
            pltpu.VMEM((5, ROWS + 2 * PAD, COLS), F32),
            pltpu.VMEM((4, ROWS, COLS), F32),
            pltpu.VMEM((group_count, ROWS, COLS), F32),
            pltpu.VMEM((3, ROWS + 2 * PAD, COLS), F32),
            pltpu.VMEM((NPSF, COLS, COLS), F32),
            pltpu.VMEM((NPSF, COLS, COLS), F32),
            pltpu.VMEM((NPSF * ROWS, GROUPS_OF_4 * COLS), BF16),
            pltpu.VMEM((GROUPS_OF_4 * COLS, NPSF * ROWS), BF16),
            pltpu.VMEM((ITEMS, 4, EXTENT, 8 * COLS), BF16),
            pltpu.VMEM((ITEMS, ROWS, COLS), F32),
            pltpu.VMEM((DEPTH, 2 * WIDE), BF16),
            pltpu.VMEM((NPSF * ROWS, 2 * WIDE), BF16),
            pltpu.VMEM((DEPTH, 2 * WIDE), F32),
            pltpu.VMEM((ITEMS, ROWS, COLS), F32),
            pltpu.VMEM((ITEMS, 4, 2, ROWS, COLS), F32),
            pltpu.VMEM((ITEMS, 2, ROWS + 8, 2 * COLS), F32),
            pltpu.VMEM((5, ROWS, COLS), F32),
            dma((6,)), dma((4,)), dma((4,)), dma((4,)), dma((4,)), dma((group_count - 1,)), dma((group_count - 1,)),
        ],
        compiler_params=pltpu.CompilerParams(
            collective_id=0, has_side_effects=True, vmem_limit_bytes=62 * 2**20
        ),
    )(item_tile, sky, psf_basis, warp_corner, warp_weight, coeff, observed, inv_var)


def solution(mesh):
    return jax.shard_map(
        per_device,
        mesh=mesh,
        in_specs=(
            P(None, "tile"),
            P("grp", None, None, None),
            P(("grp", "tile")),
            P(("grp", "tile"), None, None),
            P(("grp", "tile"), None, None, None),
            P(("grp", "tile"), None, None, None),
            P(("grp", "tile"), None, None),
            P(("grp", "tile"), None, None),
        ),
        out_specs=P(None, "tile"),
        check_vma=False,
    )
```

```python
import functools

import jax
import jax.numpy as jnp
from jax import lax
from jax.experimental import pallas as pl
from jax.experimental.pallas import tpu as pltpu
from jax.sharding import PartitionSpec as P

F32, BF16, I32 = jnp.float32, jnp.bfloat16, jnp.int32
ROWS, COLS, MARGIN, TAPS, NPSF, ITEMS = 32, 128, 24, 41, 5, 3
EXTENT = COLS + 2 * MARGIN
HALF = TAPS // 2
WIDE = ITEMS * COLS
DEPTH = TAPS * ROWS
GROUPS_OF_4 = (TAPS + 3) // 4
PAD = 8
STEP = 0.25
OFFSETS = (-2, -1, 1, 2)
SLOT = {-2: 0, -1: 1, 0: 2, 1: 3, 2: 4}


def split(value):
    high = value.astype(BF16)
    return high, (value - high.astype(F32)).astype(BF16)


def nt_dot(a, b):
    return lax.dot_general(a, b, (((1,), (1,)), ((), ())), preferred_element_type=F32)


def pack(value, right):
    lane_group = lax.broadcasted_iota(I32, (8, COLS), 1) // ROWS
    packed = jnp.zeros((8, COLS), F32)
    for i in range(4):
        turned = pltpu.roll(value[8 * i : 8 * i + 8], (32 * i + (ROWS if right else 0)) % COLS, 1)
        packed = jnp.where(lane_group == i, turned, packed)
    return packed


def unpack(packed, right):
    return jnp.concatenate(
        [pltpu.roll(packed, (-32 * i - (ROWS if right else 0)) % COLS, 1) for i in range(4)], axis=0
    )


def prepare_hot(corner, hot):
    column = lax.broadcasted_iota(I32, (EXTENT, COLS), 0)

    def hot_rows(step, _):
        n, block = step // 4, lax.rem(step, 4)
        at = corner[n, pl.ds(pl.multiple_of(block * 8, 8), 8), :]
        start = at - ((at * 23832) >> 22) * EXTENT
        for u in range(8):
            row = jnp.broadcast_to(start[u : u + 1], (EXTENT, COLS))
            hot[n, block, :, pl.ds(u * COLS, COLS)] = jnp.where(column == row, 1.0, 0.0).astype(BF16)
        return 0

    lax.fori_loop(0, ITEMS * 4, hot_rows, 0)


def prepare_taps(psf, tap_rows, tap_cols, blur_left, blur_right):
    tap_rows[...] = jnp.zeros_like(tap_rows)
    for k in range(NPSF):
        tap_rows[k, pl.ds(0, TAPS), pl.ds(0, TAPS)] = psf[0, k].astype(F32)
    for k in range(NPSF):
        tap_cols[k] = pltpu.roll(tap_rows[k], 4, 0).T
    lane_group = lax.broadcasted_iota(I32, (8, COLS), 1) // ROWS
    for j in range(GROUPS_OF_4):
        whole = []
        for k in range(NPSF):
            for r0 in range(0, ROWS, 8):
                tile = jnp.zeros((8, COLS), F32)
                for part in range(4):
                    row = jnp.broadcast_to(tap_cols[k, pl.ds(4 * j + part, 1), :], (8, COLS))
                    turned = pltpu.roll(row, (r0 + ROWS * part - HALF - 4) % COLS, 1, stride=1, stride_axis=0)
                    tile = turned if part == 0 else jnp.where(lane_group == part, turned, tile)
                whole.append(tile)
        whole = jnp.concatenate(whole, axis=0)
        blur_left[:, pl.ds(j * COLS, COLS)] = whole.astype(BF16)
        blur_right[pl.ds(j * COLS, COLS), :] = whole.T.astype(BF16)


def warp(me, count, tiles, corner, weight, region, far_in, sides, warped):
    lane = lax.broadcasted_iota(I32, (ROWS, COLS), 1)
    for t in range(3):
        left = unpack(far_in[1], True) if t == 0 else region[t, pl.ds(PAD, ROWS), :]
        right = unpack(far_in[0], False) if t == 2 else region[t + 2, pl.ds(PAD, ROWS), :]
        if t < 2:
            left = jnp.where(me - 2 + t >= 0, left, 0.0)
        if t > 0:
            right = jnp.where(me + t <= count - 1, right, 0.0)
        sides[t, pl.ds(PAD, ROWS), :] = jnp.where(lane >= COLS // 2, left, right)
    for n in range(ITEMS):
        t = jnp.clip(tiles[n] - (me - 1), 0, 2)
        for r0 in range(0, ROWS, 8):
            at = corner[n, pl.ds(r0, 8), :]
            q = (at * 23832) >> 22
            p = at - q * EXTENT
            rel = q - (lax.broadcasted_iota(I32, (8, COLS), 0) + r0) + 3
            total = jnp.zeros((8, COLS), F32)
            for dp in range(2):
                index = (p + (dp + COLS - MARGIN)) & (COLS - 1)
                middle = (p + dp >= MARGIN) & (p + dp < MARGIN + COLS)
                upper = jnp.zeros((8, COLS), F32)
                lower = jnp.zeros((8, COLS), F32)
                for o in range(8):
                    rows = pl.ds(r0 + (PAD - 3 + o), 8)
                    inside = jnp.take_along_axis(region[t + 1, rows, :], index, axis=1)
                    beside = jnp.take_along_axis(sides[t, rows, :], index, axis=1)
                    found = jnp.where(middle, inside, beside)
                    if o < 7:
                        upper = jnp.where(rel == o, found, upper)
                    if o > 0:
                        lower = jnp.where(rel == o - 1, found, lower)
                total += weight[n, dp, pl.ds(r0, 8), :].astype(F32) * upper
                total += weight[n, 2 + dp, pl.ds(r0, 8), :].astype(F32) * lower
            warped[n, pl.ds(r0, 8), :] = total


def blur(coeff, obs, ivar, warped, lifted, blur_left, misfit_parts):
    lane = lax.broadcasted_iota(I32, (ROWS, COLS), 1)
    for b in range(TAPS):
        source = lane + (b - HALF)
        inside = (source >= 0) & (source < COLS)
        for n in range(ITEMS):
            value = warped[n]
            if b != HALF:
                value = jnp.where(inside, pltpu.roll(value, (HALF - b) % COLS, 1), 0.0)
            high, low = split(value)
            lifted[pl.ds(b * ROWS, ROWS), pl.ds(n * COLS, COLS)] = high
            lifted[pl.ds(b * ROWS, ROWS), pl.ds(WIDE + n * COLS, COLS)] = low
    both = jnp.dot(blur_left[:, pl.ds(0, DEPTH)], lifted[...], preferred_element_type=F32)
    blurred = both[:, :WIDE] + both[:, WIDE:]
    for n in range(ITEMS):
        predicted = jnp.zeros((ROWS, COLS), F32)
        for k in range(NPSF):
            predicted += coeff[n, k].astype(F32) * blurred[k * ROWS : (k + 1) * ROWS, n * COLS : (n + 1) * COLS]
        misfit = ivar[n].astype(F32) * (predicted - obs[n].astype(F32))
        for k in range(NPSF):
            high, low = split(coeff[n, k].astype(F32) * misfit)
            misfit_parts[pl.ds(k * ROWS, ROWS), pl.ds(n * COLS, COLS)] = high
            misfit_parts[pl.ds(k * ROWS, ROWS), pl.ds(WIDE + n * COLS, COLS)] = low


def back(blur_right, misfit_parts, spread, backward):
    lane = lax.broadcasted_iota(I32, (ROWS, COLS), 1)
    spread[...] = jnp.dot(blur_right[pl.ds(0, DEPTH), :], misfit_parts[...], preferred_element_type=F32)
    for n in range(ITEMS):
        total = jnp.zeros((ROWS, COLS), F32)
        for b in range(TAPS):
            source = lane - (b - HALF)
            inside = (source >= 0) & (source < COLS)
            value = spread[pl.ds(b * ROWS, ROWS), pl.ds(n * COLS, COLS)]
            value += spread[pl.ds(b * ROWS, ROWS), pl.ds(WIDE + n * COLS, COLS)]
            if b != HALF:
                value = jnp.where(inside, pltpu.roll(value, (b - HALF) % COLS, 1), 0.0)
            total += value
        backward[n] = total


def scatter(corner, weight, backward, hot, parts, window_grad):
    window_grad[...] = jnp.zeros_like(window_grad)
    target = lax.broadcasted_iota(I32, (16, COLS), 0)
    for n in range(ITEMS):
        for j in range(4):
            value = weight[n, j].astype(F32) * backward[n]
            high = value.astype(BF16).astype(F32)
            parts[n, j, 0] = high
            parts[n, j, 1] = value - high
        for block in range(4):
            r0 = block * 8
            q = ((corner[n, pl.ds(r0, 8), :] * 23832) >> 22) - (r0 - 4)
            columns = []
            for u in range(8):
                row = jnp.broadcast_to(q[u : u + 1], (16, COLS))
                first, second = target == row, target == row + 1
                stack = []
                for dp in range(2):
                    for half in range(2):
                        one_up = jnp.broadcast_to(parts[n, dp, half, pl.ds(r0 + u, 1), :], (16, COLS))
                        one_low = jnp.broadcast_to(parts[n, 2 + dp, half, pl.ds(r0 + u, 1), :], (16, COLS))
                        stack.append(jnp.where(first, one_up, jnp.where(second, one_low, 0.0)).astype(BF16))
                columns.append(jnp.concatenate(stack, axis=0))
            values = jnp.concatenate(columns, axis=1)
            found = nt_dot(values, hot[n, block])
            for dp in range(2):
                part = found[dp * 32 : dp * 32 + 16] + found[dp * 32 + 16 : dp * 32 + 32]
                window_grad[n, dp, pl.ds(r0, 16), pl.ds(0, EXTENT)] += part


def gather_tiles(me, tiles, window_grad, gradient, far_gradient):
    lane = lax.broadcasted_iota(I32, (ROWS, COLS), 1)
    left_lanes = lane >= COLS // 2
    totals = [jnp.zeros((ROWS, COLS), F32) for _ in range(5)]
    for n in range(ITEMS):
        t = jnp.clip(tiles[n] - (me - 1), 0, 2)
        whole = pltpu.roll(window_grad[n, 0, pl.ds(4, ROWS), :], COLS - MARGIN, 1)
        whole += pltpu.roll(window_grad[n, 1, pl.ds(4, ROWS), :], COLS - MARGIN + 1, 1)
        beside, inside = whole[:, :COLS], whole[:, COLS:]
        left = jnp.where(left_lanes, beside, 0.0)
        right = jnp.where(left_lanes, 0.0, beside)
        for s in range(5):
            if n == 0 and s not in (1, 2, 3):
                continue
            if s - 1 in (0, 1, 2):
                totals[s] += jnp.where(t == s - 1, inside, 0.0)
            if s in (0, 1, 2):
                totals[s] += jnp.where(t == s, left, 0.0)
            if s - 2 in (0, 1, 2):
                totals[s] += jnp.where(t == s - 2, right, 0.0)
    for s in range(3):
        gradient[s] = totals[s + 1]
    far_gradient[0] = pack(totals[0], True)
    far_gradient[1] = pack(totals[4], False)


def kernel(tiles, sky_hbm, psf, corner_hbm, weight_hbm, coeff_hbm, obs_hbm, ivar_hbm, out,
           corner, weight, coeff, obs, ivar,
           region, far_out, far_in, arrived, far_arrived, sides, tap_rows, tap_cols, blur_left, blur_right,
           hot, warped, lifted, misfit_parts, spread, backward, parts, window_grad, gradient, far_gradient,
           load, near_send, near_recv, back_send, back_recv):
    me, grp = lax.axis_index("tile"), lax.axis_index("grp")
    count, group_count = lax.axis_size("tile"), lax.axis_size("grp")
    mesh_id = pl.DeviceIdType.MESH
    there = {offset: (me + offset >= 0) & (me + offset <= count - 1) for offset in OFFSETS}
    others = [lax.rem(grp + step, group_count) for step in range(group_count)]
    barrier = pltpu.get_barrier_semaphore()
    for step in range(group_count):
        for offset in OFFSETS:
            @pl.when(there[offset])
            def _():
                pl.semaphore_signal(barrier, inc=1, device_id=(others[step], me + offset), device_id_type=mesh_id)
        if step > 0:
            pl.semaphore_signal(barrier, inc=1, device_id=(others[step], me), device_id_type=mesh_id)
    sky_here = region.at[2, pl.ds(PAD, ROWS), :]
    pairs = ((sky_hbm, sky_here), (corner_hbm, corner), (weight_hbm, weight),
             (coeff_hbm, coeff), (obs_hbm, obs), (ivar_hbm, ivar))
    loads = [pltpu.make_async_copy(a, b, load.at[i]) for i, (a, b) in enumerate(pairs)]
    for copy in loads:
        copy.start()
    loads[0].wait()
    far_out[0] = pack(sky_here[...], False)
    far_out[1] = pack(sky_here[...], True)
    loads[1].wait()
    prepare_hot(corner, hot)
    neighbours = jnp.minimum(me, 2) + jnp.minimum(count - 1 - me, 2)
    pl.semaphore_wait(barrier, (neighbours + 1) * group_count - 1)

    near = []
    for number, offset in enumerate(OFFSETS):
        side = 0 if offset < 0 else 1
        near.append(pltpu.make_async_remote_copy(
            src_ref=sky_here if abs(offset) == 1 else far_out.at[side],
            dst_ref=region.at[SLOT[-offset], pl.ds(PAD, ROWS), :] if abs(offset) == 1 else far_in.at[side],
            send_sem=near_send.at[number],
            recv_sem=near_recv.at[number],
            device_id=(grp, me + offset),
            device_id_type=mesh_id,
        ))
    for number in (0, 3, 1, 2):
        pl.when(there[OFFSETS[number]])(near[number].start)
    prepare_taps(psf, tap_rows, tap_cols, blur_left, blur_right)
    for copy in loads[2:]:
        copy.wait()
    for number, offset in enumerate(OFFSETS):
        pl.when(there[-offset])(near[number].wait_recv)
    warp(me, count, tiles, corner, weight, region, far_in, sides, warped)
    blur(coeff, obs, ivar, warped, lifted, blur_left, misfit_parts)
    back(blur_right, misfit_parts, spread, backward)
    scatter(corner, weight, backward, hot, parts, window_grad)
    gather_tiles(me, tiles, window_grad, gradient, far_gradient)

    home = []
    for offset in (-2, 2, -1, 1, 0):
        for step in range(group_count):
            if offset == 0 and step == 0:
                continue
            number = OFFSETS.index(offset) if offset else 4
            if abs(offset) == 2:
                source, target = far_gradient.at[number // 3], far_arrived.at[grp, number // 3]
            else:
                source, target = gradient.at[offset + 1], arrived.at[grp, offset + 1]
            copy = pltpu.make_async_remote_copy(
                src_ref=source,
                dst_ref=target,
                send_sem=back_send.at[step, number],
                recv_sem=back_recv.at[step, number],
                device_id=(others[step], me + offset),
                device_id_type=mesh_id,
            )
            home.append((offset, copy))
            if offset == 0:
                copy.start()
            else:
                pl.when(there[offset])(copy.start)
    arrived[grp, 1] = gradient[1]
    for number, offset in enumerate(OFFSETS):
        pl.when(there[offset])(near[number].wait_send)
    for offset, copy in home:
        if offset == 0:
            copy.wait_recv()
        else:
            pl.when(there[-offset])(copy.wait_recv)
    lane = lax.broadcasted_iota(I32, (ROWS, COLS), 1)
    total = jnp.zeros((ROWS, COLS), F32)
    for g in range(group_count):
        total += arrived[g, 1]
        total += jnp.where(there[1], arrived[g, 0], 0.0)
        total += jnp.where(there[-1], arrived[g, 2], 0.0)
        total += jnp.where(there[2] & (lane >= COLS - ROWS), unpack(far_arrived[g, 0], True), 0.0)
        total += jnp.where(there[-2] & (lane < ROWS), unpack(far_arrived[g, 1], False), 0.0)
    out[...] = sky_here[...] - STEP * total
    for offset, copy in home:
        if offset == 0:
            copy.wait_send()
        else:
            pl.when(there[offset])(copy.wait_send)


def per_device(sky, psf_basis, item_tile, warp_corner, warp_weight, psf_coeff, observed, inv_var):
    group_count = lax.axis_size("grp")
    vmem = pl.BlockSpec(memory_space=pltpu.VMEM)
    dma = pltpu.SemaphoreType.DMA
    hbm = pl.BlockSpec(memory_space=pltpu.HBM)
    coeff = psf_coeff.transpose(0, 2, 1, 3)
    return pl.pallas_call(
        kernel,
        out_shape=jax.ShapeDtypeStruct((ROWS, COLS), F32),
        in_specs=[pl.BlockSpec(memory_space=pltpu.SMEM), hbm, vmem] + [hbm] * 5,
        out_specs=vmem,
        scratch_shapes=[
            pltpu.VMEM(warp_corner.shape, I32),
            pltpu.VMEM(warp_weight.shape, BF16),
            pltpu.VMEM(coeff.shape, BF16),
            pltpu.VMEM(observed.shape, BF16),
            pltpu.VMEM(inv_var.shape, BF16),
            pltpu.VMEM((5, ROWS + 2 * PAD, COLS), F32),
            pltpu.VMEM((2, 8, COLS), F32),
            pltpu.VMEM((2, 8, COLS), F32),
            pltpu.VMEM((group_count, 3, ROWS, COLS), F32),
            pltpu.VMEM((group_count, 2, 8, COLS), F32),
            pltpu.VMEM((3, ROWS + 2 * PAD, COLS), F32),
            pltpu.VMEM((NPSF, COLS, COLS), F32),
            pltpu.VMEM((NPSF, COLS, COLS), F32),
            pltpu.VMEM((NPSF * ROWS, GROUPS_OF_4 * COLS), BF16),
            pltpu.VMEM((GROUPS_OF_4 * COLS, NPSF * ROWS), BF16),
            pltpu.VMEM((ITEMS, 4, EXTENT, 8 * COLS), BF16),
            pltpu.VMEM((ITEMS, ROWS, COLS), F32),
            pltpu.VMEM((DEPTH, 2 * WIDE), BF16),
            pltpu.VMEM((NPSF * ROWS, 2 * WIDE), BF16),
            pltpu.VMEM((DEPTH, 2 * WIDE), F32),
            pltpu.VMEM((ITEMS, ROWS, COLS), F32),
            pltpu.VMEM((ITEMS, 4, 2, ROWS, COLS), F32),
            pltpu.VMEM((ITEMS, 2, ROWS + 8, 2 * COLS), F32),
            pltpu.VMEM((3, ROWS, COLS), F32),
            pltpu.VMEM((2, 8, COLS), F32),
            dma((6,)), dma((4,)), dma((4,)), dma((group_count, 5)), dma((group_count, 5)),
        ],
        compiler_params=pltpu.CompilerParams(
            collective_id=0, has_side_effects=True, vmem_limit_bytes=62 * 2**20
        ),
    )(item_tile, sky, psf_basis, warp_corner, warp_weight, coeff, observed, inv_var)


def solution(mesh):
    return jax.shard_map(
        per_device,
        mesh=mesh,
        in_specs=(
            P(None, "tile"),
            P("grp", None, None, None),
            P(("grp", "tile")),
            P(("grp", "tile"), None, None),
            P(("grp", "tile"), None, None, None),
            P(("grp", "tile"), None, None, None),
            P(("grp", "tile"), None, None),
            P(("grp", "tile"), None, None),
        ),
        out_specs=P(None, "tile"),
        check_vma=False,
    )
```

```python
import jax
import jax.numpy as jnp
from jax import lax
from jax.experimental import pallas as pl
from jax.experimental.pallas import tpu as pltpu
from jax.sharding import PartitionSpec as P

F32, BF16, I32 = jnp.float32, jnp.bfloat16, jnp.int32
ROWS, COLS, MARGIN, TAPS, NPSF, ITEMS = 32, 128, 24, 41, 5, 3
EXTENT = COLS + 2 * MARGIN
HALF = TAPS // 2
WIDE = ITEMS * COLS
DEPTH = TAPS * ROWS
GROUPS_OF_4 = (TAPS + 3) // 4
PAD = 8
STEP = 0.25
OFFSETS = (-2, -1, 1, 2)
SLOT = {-2: 0, -1: 1, 0: 2, 1: 3, 2: 4}


def split(value):
    high = value.astype(BF16)
    return high, (value - high.astype(F32)).astype(BF16)


def nt_dot(a, b):
    return lax.dot_general(a, b, (((1,), (1,)), ((), ())), preferred_element_type=F32)


def pack(value, right):
    lane_group = lax.broadcasted_iota(I32, (8, COLS), 1) // ROWS
    packed = jnp.zeros((8, COLS), F32)
    for i in range(4):
        turned = pltpu.roll(value[8 * i : 8 * i + 8], (32 * i + (ROWS if right else 0)) % COLS, 1)
        packed = jnp.where(lane_group == i, turned, packed)
    return packed


def unpack(packed, right):
    return jnp.concatenate(
        [pltpu.roll(packed, (-32 * i - (ROWS if right else 0)) % COLS, 1) for i in range(4)], axis=0
    )


def prepare_hot(corner, hot):
    column = lax.broadcasted_iota(I32, (EXTENT, COLS), 0)

    def hot_rows(step, _):
        n, block = step // 4, lax.rem(step, 4)
        at = corner[n, pl.ds(pl.multiple_of(block * 8, 8), 8), :]
        start = at - ((at * 23832) >> 22) * EXTENT
        for u in range(8):
            row = jnp.broadcast_to(start[u : u + 1], (EXTENT, COLS))
            hot[n, block, :, pl.ds(u * COLS, COLS)] = jnp.where(column == row, 1.0, 0.0).astype(BF16)
        return 0

    lax.fori_loop(0, ITEMS * 4, hot_rows, 0)


def prepare_taps(psf, tap_rows, tap_cols, blur_left, blur_right):
    tap_rows[...] = jnp.zeros_like(tap_rows)
    for k in range(NPSF):
        tap_rows[k, pl.ds(0, TAPS), pl.ds(0, TAPS)] = psf[0, k].astype(F32)
    for k in range(NPSF):
        tap_cols[k] = pltpu.roll(tap_rows[k], 4, 0).T
    lane_group = lax.broadcasted_iota(I32, (8, COLS), 1) // ROWS
    for j in range(GROUPS_OF_4):
        whole = []
        for k in range(NPSF):
            for r0 in range(0, ROWS, 8):
                tile = jnp.zeros((8, COLS), F32)
                for part in range(4):
                    row = jnp.broadcast_to(tap_cols[k, pl.ds(4 * j + part, 1), :], (8, COLS))
                    turned = pltpu.roll(row, (r0 + ROWS * part - HALF - 4) % COLS, 1, stride=1, stride_axis=0)
                    tile = turned if part == 0 else jnp.where(lane_group == part, turned, tile)
                whole.append(tile)
        whole = jnp.concatenate(whole, axis=0)
        blur_left[:, pl.ds(j * COLS, COLS)] = whole.astype(BF16)
        blur_right[pl.ds(j * COLS, COLS), :] = whole.T.astype(BF16)


def join_sides(me, count, region, far_in, sides):
    lane = lax.broadcasted_iota(I32, (ROWS, COLS), 1)
    for t in range(3):
        left = unpack(far_in[1], True) if t == 0 else region[t, pl.ds(PAD, ROWS), :]
        right = unpack(far_in[0], False) if t == 2 else region[t + 2, pl.ds(PAD, ROWS), :]
        if t < 2:
            left = jnp.where(me - 2 + t >= 0, left, 0.0)
        if t > 0:
            right = jnp.where(me + t <= count - 1, right, 0.0)
        sides[t, pl.ds(PAD, ROWS), :] = jnp.where(lane >= COLS // 2, left, right)


def warp(n, me, tiles, corner, weight, region, sides, warped):
    t = jnp.clip(tiles[n] - (me - 1), 0, 2)
    for r0 in range(0, ROWS, 8):
        at = corner[n, pl.ds(r0, 8), :]
        q = (at * 23832) >> 22
        p = at - q * EXTENT
        rel = q - (lax.broadcasted_iota(I32, (8, COLS), 0) + r0) + 3
        total = jnp.zeros((8, COLS), F32)
        for dp in range(2):
            index = (p + (dp + COLS - MARGIN)) & (COLS - 1)
            middle = (p + dp >= MARGIN) & (p + dp < MARGIN + COLS)
            upper = jnp.zeros((8, COLS), F32)
            lower = jnp.zeros((8, COLS), F32)
            for o in range(8):
                rows = pl.ds(r0 + (PAD - 3 + o), 8)
                inside = jnp.take_along_axis(region[t + 1, rows, :], index, axis=1)
                beside = jnp.take_along_axis(sides[t, rows, :], index, axis=1)
                found = jnp.where(middle, inside, beside)
                if o < 7:
                    upper = jnp.where(rel == o, found, upper)
                if o > 0:
                    lower = jnp.where(rel == o - 1, found, lower)
            total += weight[n, dp, pl.ds(r0, 8), :].astype(F32) * upper
            total += weight[n, 2 + dp, pl.ds(r0, 8), :].astype(F32) * lower
        warped[n, pl.ds(r0, 8), :] = total


def blur(n, coeff, obs, ivar, warped, lifted, blur_left, misfit_parts):
    lane = lax.broadcasted_iota(I32, (ROWS, COLS), 1)
    for b in range(TAPS):
        source = lane + (b - HALF)
        inside = (source >= 0) & (source < COLS)
        value = warped[n]
        if b != HALF:
            value = jnp.where(inside, pltpu.roll(value, (HALF - b) % COLS, 1), 0.0)
        high, low = split(value)
        lifted[n, pl.ds(b * ROWS, ROWS), pl.ds(0, COLS)] = high
        lifted[n, pl.ds(b * ROWS, ROWS), pl.ds(COLS, COLS)] = low
    both = jnp.dot(blur_left[:, pl.ds(0, DEPTH)], lifted[n], preferred_element_type=F32)
    blurred = both[:, :COLS] + both[:, COLS:]
    predicted = jnp.zeros((ROWS, COLS), F32)
    for k in range(NPSF):
        predicted += coeff[n, k].astype(F32) * blurred[k * ROWS : (k + 1) * ROWS]
    misfit = ivar[n].astype(F32) * (predicted - obs[n].astype(F32))
    for k in range(NPSF):
        high, low = split(coeff[n, k].astype(F32) * misfit)
        misfit_parts[n, pl.ds(k * ROWS, ROWS), pl.ds(0, COLS)] = high
        misfit_parts[n, pl.ds(k * ROWS, ROWS), pl.ds(COLS, COLS)] = low


def back(n, blur_right, misfit_parts, spread, backward):
    lane = lax.broadcasted_iota(I32, (ROWS, COLS), 1)
    spread[n] = jnp.dot(blur_right[pl.ds(0, DEPTH), :], misfit_parts[n], preferred_element_type=F32)
    total = jnp.zeros((ROWS, COLS), F32)
    for b in range(TAPS):
        source = lane - (b - HALF)
        inside = (source >= 0) & (source < COLS)
        value = spread[n, pl.ds(b * ROWS, ROWS), pl.ds(0, COLS)] + spread[n, pl.ds(b * ROWS, ROWS), pl.ds(COLS, COLS)]
        if b != HALF:
            value = jnp.where(inside, pltpu.roll(value, (b - HALF) % COLS, 1), 0.0)
        total += value
    backward[n] = total


def scatter(n, corner, weight, backward, hot, parts, window_grad):
    target = lax.broadcasted_iota(I32, (16, COLS), 0)
    for j in range(4):
        value = weight[n, j].astype(F32) * backward[n]
        high = value.astype(BF16).astype(F32)
        parts[n, j, 0] = high
        parts[n, j, 1] = value - high
    for block in range(4):
        r0 = block * 8
        q = ((corner[n, pl.ds(r0, 8), :] * 23832) >> 22) - (r0 - 4)
        columns = []
        for u in range(8):
            row = jnp.broadcast_to(q[u : u + 1], (16, COLS))
            first, second = target == row, target == row + 1
            stack = []
            for dp in range(2):
                for half in range(2):
                    one_up = jnp.broadcast_to(parts[n, dp, half, pl.ds(r0 + u, 1), :], (16, COLS))
                    one_low = jnp.broadcast_to(parts[n, 2 + dp, half, pl.ds(r0 + u, 1), :], (16, COLS))
                    stack.append(jnp.where(first, one_up, jnp.where(second, one_low, 0.0)).astype(BF16))
            columns.append(jnp.concatenate(stack, axis=0))
        values = jnp.concatenate(columns, axis=1)
        found = nt_dot(values, hot[n, block])
        for dp in range(2):
            part = found[dp * 32 : dp * 32 + 16] + found[dp * 32 + 16 : dp * 32 + 32]
            window_grad[n, dp, pl.ds(r0, 16), pl.ds(0, EXTENT)] += part


def gather_tiles(me, tiles, window_grad, gradient, far_gradient):
    lane = lax.broadcasted_iota(I32, (ROWS, COLS), 1)
    left_lanes = lane >= COLS // 2
    totals = [jnp.zeros((ROWS, COLS), F32) for _ in range(5)]
    for n in range(ITEMS):
        t = jnp.clip(tiles[n] - (me - 1), 0, 2)
        whole = pltpu.roll(window_grad[n, 0, pl.ds(4, ROWS), :], COLS - MARGIN, 1)
        whole += pltpu.roll(window_grad[n, 1, pl.ds(4, ROWS), :], COLS - MARGIN + 1, 1)
        beside, inside = whole[:, :COLS], whole[:, COLS:]
        left = jnp.where(left_lanes, beside, 0.0)
        right = jnp.where(left_lanes, 0.0, beside)
        for s in range(5):
            if n == 0 and s not in (1, 2, 3):
                continue
            if s - 1 in (0, 1, 2):
                totals[s] += jnp.where(t == s - 1, inside, 0.0)
            if s in (0, 1, 2):
                totals[s] += jnp.where(t == s, left, 0.0)
            if s - 2 in (0, 1, 2):
                totals[s] += jnp.where(t == s - 2, right, 0.0)
    for s in range(3):
        gradient[s] = totals[s + 1]
    far_gradient[0] = pack(totals[0], True)
    far_gradient[1] = pack(totals[4], False)


def kernel(tiles_hbm, sky_hbm, psf_hbm, corner_hbm, weight_hbm, coeff_hbm, obs_hbm, ivar_hbm, out,
           tiles, psf, corner, weight, coeff, obs, ivar,
           region, far_out, far_in, arrived, far_arrived, sides, tap_rows, tap_cols, blur_left, blur_right,
           hot, warped, lifted, misfit_parts, spread, backward, parts, window_grad, gradient, far_gradient,
           load, near_send, near_recv, back_send, back_recv, ready):
    me, grp = lax.axis_index("tile"), lax.axis_index("grp")
    count, group_count = lax.axis_size("tile"), lax.axis_size("grp")
    mesh_id = pl.DeviceIdType.MESH
    there = {offset: (me + offset >= 0) & (me + offset <= count - 1) for offset in OFFSETS}
    others = [lax.rem(grp + step, group_count) for step in range(group_count)]
    barrier = pltpu.get_barrier_semaphore()
    for offset in OFFSETS:
        @pl.when(there[offset])
        def _():
            pl.semaphore_signal(barrier, inc=1, device_id=(grp, me + offset), device_id_type=mesh_id)
    for other in others[1:]:
        pl.semaphore_signal(barrier, inc=1, device_id=(other, me), device_id_type=mesh_id)
    sky_here = region.at[2, pl.ds(PAD, ROWS), :]
    pairs = ((sky_hbm, sky_here), (corner_hbm, corner), (weight_hbm, weight),
             (coeff_hbm, coeff), (obs_hbm, obs), (ivar_hbm, ivar), (tiles_hbm, tiles), (psf_hbm, psf))
    loads = [pltpu.make_async_copy(a, b, load.at[i]) for i, (a, b) in enumerate(pairs)]
    for copy in loads:
        copy.start()
    loads[0].wait()
    far_out[0] = pack(sky_here[...], False)
    far_out[1] = pack(sky_here[...], True)
    loads[1].wait()
    prepare_hot(corner, hot)
    neighbours = jnp.minimum(me, 2) + jnp.minimum(count - 1 - me, 2)
    pl.semaphore_wait(barrier, neighbours + group_count - 1)

    near = []
    for number, offset in enumerate(OFFSETS):
        side = 0 if offset < 0 else 1
        near.append(pltpu.make_async_remote_copy(
            src_ref=sky_here if abs(offset) == 1 else far_out.at[side],
            dst_ref=region.at[SLOT[-offset], pl.ds(PAD, ROWS), :] if abs(offset) == 1 else far_in.at[side],
            send_sem=near_send.at[number],
            recv_sem=near_recv.at[number],
            device_id=(grp, me + offset),
            device_id_type=mesh_id,
        ))
    for number in (0, 3, 1, 2):
        pl.when(there[OFFSETS[number]])(near[number].start)
    for step, other in enumerate(others[1:]):
        pl.semaphore_signal(ready.at[step], inc=1, device_id=(other, me), device_id_type=mesh_id)
    window_grad[...] = jnp.zeros_like(window_grad)
    loads[7].wait()
    prepare_taps(psf, tap_rows, tap_cols, blur_left, blur_right)
    for copy in loads[2:7]:
        copy.wait()
    for number, offset in enumerate(OFFSETS):
        pl.when(there[-offset])(near[number].wait_recv)
    for step in range(group_count - 1):
        pl.semaphore_wait(ready.at[step], 1)
    join_sides(me, count, region, far_in, sides)
    for n in range(ITEMS):
        warp(n, me, tiles, corner, weight, region, sides, warped)
    for n in range(ITEMS):
        blur(n, coeff, obs, ivar, warped, lifted, blur_left, misfit_parts)
    for n in range(ITEMS):
        back(n, blur_right, misfit_parts, spread, backward)
    for n in range(ITEMS):
        scatter(n, corner, weight, backward, hot, parts, window_grad)
    gather_tiles(me, tiles, window_grad, gradient, far_gradient)

    home = {}
    for offset in (-2, 2, -1, 1, 0):
        number = OFFSETS.index(offset) if offset else 4
        if abs(offset) == 2:
            source, target = far_gradient.at[number // 3], far_arrived.at[grp, number // 3]
        else:
            source, target = gradient.at[offset + 1], arrived.at[grp, offset + 1]
        home[offset] = [
            pltpu.make_async_remote_copy(
                src_ref=source,
                dst_ref=target,
                send_sem=back_send.at[step, number],
                recv_sem=back_recv.at[step, number],
                device_id=(others[step], me + offset),
                device_id_type=mesh_id,
            )
            for step in range(0 if offset else 1, group_count)
        ]

        def leave_for(offset=offset):
            for copy in home[offset]:
                copy.start()

        if offset:
            pl.when(there[offset])(leave_for)
        else:
            leave_for()
    arrived[grp, 1] = gradient[1]
    for number, offset in enumerate(OFFSETS):
        pl.when(there[offset])(near[number].wait_send)
    for offset in (0, *OFFSETS):
        def arrive(offset=offset):
            for copy in home[offset]:
                copy.wait_recv()

        if offset:
            pl.when(there[-offset])(arrive)
        else:
            arrive()
    lane = lax.broadcasted_iota(I32, (ROWS, COLS), 1)
    total = jnp.zeros((ROWS, COLS), F32)
    for g in range(group_count):
        total += arrived[g, 1]
        total += jnp.where(there[1], arrived[g, 0], 0.0)
        total += jnp.where(there[-1], arrived[g, 2], 0.0)
        total += jnp.where(there[2] & (lane >= COLS - ROWS), unpack(far_arrived[g, 0], True), 0.0)
        total += jnp.where(there[-2] & (lane < ROWS), unpack(far_arrived[g, 1], False), 0.0)
    out[...] = sky_here[...] - STEP * total
    for offset in (0, *OFFSETS):
        def leave(offset=offset):
            for copy in home[offset]:
                copy.wait_send()

        if offset:
            pl.when(there[offset])(leave)
        else:
            leave()


def per_device(sky, psf_basis, item_tile, warp_corner, warp_weight, psf_coeff, observed, inv_var):
    group_count = lax.axis_size("grp")
    vmem = pl.BlockSpec(memory_space=pltpu.VMEM)
    dma = pltpu.SemaphoreType.DMA
    hbm = pl.BlockSpec(memory_space=pltpu.HBM)
    coeff = psf_coeff.transpose(0, 2, 1, 3)
    return pl.pallas_call(
        kernel,
        out_shape=jax.ShapeDtypeStruct((ROWS, COLS), F32),
        in_specs=[hbm] * 8,
        out_specs=vmem,
        scratch_shapes=[
            pltpu.SMEM(item_tile.shape, I32),
            pltpu.VMEM(psf_basis.shape, BF16),
            pltpu.VMEM(warp_corner.shape, I32),
            pltpu.VMEM(warp_weight.shape, BF16),
            pltpu.VMEM(coeff.shape, BF16),
            pltpu.VMEM(observed.shape, BF16),
            pltpu.VMEM(inv_var.shape, BF16),
            pltpu.VMEM((5, ROWS + 2 * PAD, COLS), F32),
            pltpu.VMEM((2, 8, COLS), F32),
            pltpu.VMEM((2, 8, COLS), F32),
            pltpu.VMEM((group_count, 3, ROWS, COLS), F32),
            pltpu.VMEM((group_count, 2, 8, COLS), F32),
            pltpu.VMEM((3, ROWS + 2 * PAD, COLS), F32),
            pltpu.VMEM((NPSF, COLS, COLS), F32),
            pltpu.VMEM((NPSF, COLS, COLS), F32),
            pltpu.VMEM((NPSF * ROWS, GROUPS_OF_4 * COLS), BF16),
            pltpu.VMEM((GROUPS_OF_4 * COLS, NPSF * ROWS), BF16),
            pltpu.VMEM((ITEMS, 4, EXTENT, 8 * COLS), BF16),
            pltpu.VMEM((ITEMS, ROWS, COLS), F32),
            pltpu.VMEM((ITEMS, DEPTH, 2 * COLS), BF16),
            pltpu.VMEM((ITEMS, NPSF * ROWS, 2 * COLS), BF16),
            pltpu.VMEM((ITEMS, DEPTH, 2 * COLS), F32),
            pltpu.VMEM((ITEMS, ROWS, COLS), F32),
            pltpu.VMEM((ITEMS, 4, 2, ROWS, COLS), F32),
            pltpu.VMEM((ITEMS, 2, ROWS + 8, 2 * COLS), F32),
            pltpu.VMEM((3, ROWS, COLS), F32),
            pltpu.VMEM((2, 8, COLS), F32),
            dma((8,)), dma((4,)), dma((4,)), dma((group_count, 5)), dma((group_count, 5)),
            pltpu.SemaphoreType.REGULAR((group_count - 1,)),
        ],
        compiler_params=pltpu.CompilerParams(
            collective_id=0, has_side_effects=True, vmem_limit_bytes=int(53.91 * 2**20)
        ),
    )(item_tile, sky, psf_basis, warp_corner, warp_weight, coeff, observed, inv_var)


def solution(mesh):
    return jax.shard_map(
        per_device,
        mesh=mesh,
        in_specs=(
            P(None, "tile"),
            P("grp", None, None, None),
            P(("grp", "tile")),
            P(("grp", "tile"), None, None),
            P(("grp", "tile"), None, None, None),
            P(("grp", "tile"), None, None, None),
            P(("grp", "tile"), None, None),
            P(("grp", "tile"), None, None),
        ),
        out_specs=P(None, "tile"),
        check_vma=False,
    )
```

```python
import functools

import jax
import jax.numpy as jnp
from jax import lax
from jax.experimental import pallas as pl
from jax.experimental.pallas import tpu as pltpu
from jax.sharding import PartitionSpec as P

F32, BF16, I32 = jnp.float32, jnp.bfloat16, jnp.int32
ROWS, COLS, MARGIN, TAPS, NPSF, ITEMS = 32, 128, 24, 41, 5, 3
EXTENT = COLS + 2 * MARGIN
HALF = TAPS // 2
WIDE = ITEMS * COLS
DEPTH = TAPS * ROWS
GROUPS_OF_4 = (TAPS + 3) // 4
PAD = 8
STEP = 0.25
OFFSETS = (-2, -1, 1, 2)
SLOT = {-2: 0, -1: 1, 0: 2, 1: 3, 2: 4}


def split(value):
    high = value.astype(BF16)
    return high, (value - high.astype(F32)).astype(BF16)


def nt_dot(a, b):
    return lax.dot_general(a, b, (((1,), (1,)), ((), ())), preferred_element_type=F32)


def pack(value, right):
    lane_group = lax.broadcasted_iota(I32, (8, COLS), 1) // ROWS
    packed = jnp.zeros((8, COLS), F32)
    for i in range(4):
        turned = pltpu.roll(value[8 * i : 8 * i + 8], (32 * i + (ROWS if right else 0)) % COLS, 1)
        packed = jnp.where(lane_group == i, turned, packed)
    return packed


def unpack(packed, right):
    return jnp.concatenate(
        [pltpu.roll(packed, (-32 * i - (ROWS if right else 0)) % COLS, 1) for i in range(4)], axis=0
    )


def prepare_hot(corner, hot):
    column = lax.broadcasted_iota(I32, (EXTENT, COLS), 0)

    def hot_rows(step, _):
        n, block = step // 4, lax.rem(step, 4)
        at = corner[n, pl.ds(pl.multiple_of(block * 8, 8), 8), :]
        start = at - ((at * 23832) >> 22) * EXTENT
        for u in range(8):
            row = jnp.broadcast_to(start[u : u + 1], (EXTENT, COLS))
            hot[n, block, :, pl.ds(u * COLS, COLS)] = jnp.where(column == row, 1.0, 0.0).astype(BF16)
        return 0

    lax.fori_loop(0, ITEMS * 4, hot_rows, 0)


def prepare_taps(psf, tap_rows, tap_cols, blur_left, blur_right):
    tap_rows[...] = jnp.zeros_like(tap_rows)
    for k in range(NPSF):
        tap_rows[k, pl.ds(0, TAPS), pl.ds(0, TAPS)] = psf[0, k].astype(F32)
    for k in range(NPSF):
        tap_cols[k] = pltpu.roll(tap_rows[k], 4, 0).T
    lane_group = lax.broadcasted_iota(I32, (8, COLS), 1) // ROWS
    for j in range(GROUPS_OF_4):
        whole = []
        for k in range(NPSF):
            for r0 in range(0, ROWS, 8):
                tile = jnp.zeros((8, COLS), F32)
                for part in range(4):
                    row = jnp.broadcast_to(tap_cols[k, pl.ds(4 * j + part, 1), :], (8, COLS))
                    turned = pltpu.roll(row, (r0 + ROWS * part - HALF - 4) % COLS, 1, stride=1, stride_axis=0)
                    tile = turned if part == 0 else jnp.where(lane_group == part, turned, tile)
                whole.append(tile)
        whole = jnp.concatenate(whole, axis=0)
        blur_left[:, pl.ds(j * COLS, COLS)] = whole.astype(BF16)
        blur_right[pl.ds(j * COLS, COLS), :] = whole.T.astype(BF16)


def join_sides(me, count, region, far_in, sides):
    lane = lax.broadcasted_iota(I32, (ROWS, COLS), 1)
    for t in range(3):
        left = unpack(far_in[1], True) if t == 0 else region[t, pl.ds(PAD, ROWS), :]
        right = unpack(far_in[0], False) if t == 2 else region[t + 2, pl.ds(PAD, ROWS), :]
        if t < 2:
            left = jnp.where(me - 2 + t >= 0, left, 0.0)
        if t > 0:
            right = jnp.where(me + t <= count - 1, right, 0.0)
        sides[t, pl.ds(PAD, ROWS), :] = jnp.where(lane >= COLS // 2, left, right)


def warp(n, me, tiles, corner, weight, region, sides, warped):
    t = jnp.clip(tiles[n] - (me - 1), 0, 2)
    for r0 in range(0, ROWS, 8):
        at = corner[n, pl.ds(r0, 8), :]
        q = (at * 23832) >> 22
        p = at - q * EXTENT
        rel = q - (lax.broadcasted_iota(I32, (8, COLS), 0) + r0) + 3
        total = jnp.zeros((8, COLS), F32)
        for dp in range(2):
            index = (p + (dp + COLS - MARGIN)) & (COLS - 1)
            middle = (p + dp >= MARGIN) & (p + dp < MARGIN + COLS)
            upper = jnp.zeros((8, COLS), F32)
            lower = jnp.zeros((8, COLS), F32)
            for o in range(8):
                rows = pl.ds(r0 + (PAD - 3 + o), 8)
                inside = jnp.take_along_axis(region[t + 1, rows, :], index, axis=1)
                beside = jnp.take_along_axis(sides[t, rows, :], index, axis=1)
                found = jnp.where(middle, inside, beside)
                if o < 7:
                    upper = jnp.where(rel == o, found, upper)
                if o > 0:
                    lower = jnp.where(rel == o - 1, found, lower)
            total += weight[n, dp, pl.ds(r0, 8), :].astype(F32) * upper
            total += weight[n, 2 + dp, pl.ds(r0, 8), :].astype(F32) * lower
        warped[n, pl.ds(r0, 8), :] = total


def blur(n, coeff, obs, ivar, warped, lifted, blur_left, misfit_parts):
    lane = lax.broadcasted_iota(I32, (ROWS, COLS), 1)
    for b in range(TAPS):
        source = lane + (b - HALF)
        inside = (source >= 0) & (source < COLS)
        value = warped[n]
        if b != HALF:
            value = jnp.where(inside, pltpu.roll(value, (HALF - b) % COLS, 1), 0.0)
        high, low = split(value)
        lifted[n, pl.ds(b * ROWS, ROWS), pl.ds(0, COLS)] = high
        lifted[n, pl.ds(b * ROWS, ROWS), pl.ds(COLS, COLS)] = low
    both = jnp.dot(blur_left[:, pl.ds(0, DEPTH)], lifted[n], preferred_element_type=F32)
    blurred = both[:, :COLS] + both[:, COLS:]
    predicted = jnp.zeros((ROWS, COLS), F32)
    for k in range(NPSF):
        predicted += coeff[n, k].astype(F32) * blurred[k * ROWS : (k + 1) * ROWS]
    misfit = ivar[n].astype(F32) * (predicted - obs[n].astype(F32))
    for k in range(NPSF):
        high, low = split(coeff[n, k].astype(F32) * misfit)
        misfit_parts[n, pl.ds(k * ROWS, ROWS), pl.ds(0, COLS)] = high
        misfit_parts[n, pl.ds(k * ROWS, ROWS), pl.ds(COLS, COLS)] = low


def back(n, blur_right, misfit_parts, spread, backward):
    lane = lax.broadcasted_iota(I32, (ROWS, COLS), 1)
    spread[n] = jnp.dot(blur_right[pl.ds(0, DEPTH), :], misfit_parts[n], preferred_element_type=F32)
    total = jnp.zeros((ROWS, COLS), F32)
    for b in range(TAPS):
        source = lane - (b - HALF)
        inside = (source >= 0) & (source < COLS)
        value = spread[n, pl.ds(b * ROWS, ROWS), pl.ds(0, COLS)] + spread[n, pl.ds(b * ROWS, ROWS), pl.ds(COLS, COLS)]
        if b != HALF:
            value = jnp.where(inside, pltpu.roll(value, (b - HALF) % COLS, 1), 0.0)
        total += value
    backward[n] = total


def scatter(n, corner, weight, backward, hot, parts, window_grad):
    target = lax.broadcasted_iota(I32, (16, COLS), 0)
    for j in range(4):
        value = weight[n, j].astype(F32) * backward[n]
        high = value.astype(BF16).astype(F32)
        parts[n, j, 0] = high
        parts[n, j, 1] = value - high
    for block in range(4):
        r0 = block * 8
        q = ((corner[n, pl.ds(r0, 8), :] * 23832) >> 22) - (r0 - 4)
        columns = []
        for u in range(8):
            row = jnp.broadcast_to(q[u : u + 1], (16, COLS))
            first, second = target == row, target == row + 1
            stack = []
            for dp in range(2):
                for half in range(2):
                    one_up = jnp.broadcast_to(parts[n, dp, half, pl.ds(r0 + u, 1), :], (16, COLS))
                    one_low = jnp.broadcast_to(parts[n, 2 + dp, half, pl.ds(r0 + u, 1), :], (16, COLS))
                    stack.append(jnp.where(first, one_up, jnp.where(second, one_low, 0.0)).astype(BF16))
            columns.append(jnp.concatenate(stack, axis=0))
        values = jnp.concatenate(columns, axis=1)
        found = nt_dot(values, hot[n, block])
        for dp in range(2):
            part = found[dp * 32 : dp * 32 + 16] + found[dp * 32 + 16 : dp * 32 + 32]
            window_grad[n, dp, pl.ds(r0, 16), pl.ds(0, EXTENT)] += part


def gather_tiles(me, tiles, window_grad, gradient, far_gradient):
    lane = lax.broadcasted_iota(I32, (ROWS, COLS), 1)
    left_lanes = lane >= COLS // 2
    totals = [jnp.zeros((ROWS, COLS), F32) for _ in range(5)]
    for n in range(ITEMS):
        t = jnp.clip(tiles[n] - (me - 1), 0, 2)
        whole = pltpu.roll(window_grad[n, 0, pl.ds(4, ROWS), :], COLS - MARGIN, 1)
        whole += pltpu.roll(window_grad[n, 1, pl.ds(4, ROWS), :], COLS - MARGIN + 1, 1)
        beside, inside = whole[:, :COLS], whole[:, COLS:]
        left = jnp.where(left_lanes, beside, 0.0)
        right = jnp.where(left_lanes, 0.0, beside)
        for s in range(5):
            if n == 0 and s not in (1, 2, 3):
                continue
            if s - 1 in (0, 1, 2):
                totals[s] += jnp.where(t == s - 1, inside, 0.0)
            if s in (0, 1, 2):
                totals[s] += jnp.where(t == s, left, 0.0)
            if s - 2 in (0, 1, 2):
                totals[s] += jnp.where(t == s - 2, right, 0.0)
    for s in range(3):
        gradient[s] = totals[s + 1]
    far_gradient[0] = pack(totals[0], True)
    far_gradient[1] = pack(totals[4], False)


def kernel(tiles_hbm, sky_hbm, psf_hbm, corner_hbm, weight_hbm, coeff_hbm, obs_hbm, ivar_hbm, out,
           tiles, psf, corner, weight, coeff, obs, ivar,
           region, far_out, far_in, arrived, far_arrived, sides, tap_rows, tap_cols, blur_left, blur_right,
           hot, warped, lifted, misfit_parts, spread, backward, parts, window_grad, gradient, far_gradient,
           load, near_send, near_recv, back_send, back_recv, ready):
    me, grp = lax.axis_index("tile"), lax.axis_index("grp")
    count, group_count = lax.axis_size("tile"), lax.axis_size("grp")
    mesh_id = pl.DeviceIdType.MESH
    there = {offset: (me + offset >= 0) & (me + offset <= count - 1) for offset in OFFSETS}
    others = [lax.rem(grp + step, group_count) for step in range(group_count)]
    barrier = pltpu.get_barrier_semaphore()
    for offset in OFFSETS:
        @pl.when(there[offset])
        def _():
            pl.semaphore_signal(barrier, inc=1, device_id=(grp, me + offset), device_id_type=mesh_id)
    for other in others[1:]:
        pl.semaphore_signal(barrier, inc=1, device_id=(other, me), device_id_type=mesh_id)
    sky_here = region.at[2, pl.ds(PAD, ROWS), :]
    pairs = ((sky_hbm, sky_here), (corner_hbm, corner), (weight_hbm, weight),
             (coeff_hbm, coeff), (obs_hbm, obs), (ivar_hbm, ivar), (tiles_hbm, tiles), (psf_hbm, psf))
    loads = [pltpu.make_async_copy(a, b, load.at[i]) for i, (a, b) in enumerate(pairs)]
    for copy in loads:
        copy.start()
    loads[0].wait()
    far_out[0] = pack(sky_here[...], False)
    far_out[1] = pack(sky_here[...], True)
    neighbours = jnp.minimum(me, 2) + jnp.minimum(count - 1 - me, 2)
    pl.semaphore_wait(barrier, neighbours + group_count - 1)

    near = []
    for number, offset in enumerate(OFFSETS):
        side = 0 if offset < 0 else 1
        near.append(pltpu.make_async_remote_copy(
            src_ref=sky_here if abs(offset) == 1 else far_out.at[side],
            dst_ref=region.at[SLOT[-offset], pl.ds(PAD, ROWS), :] if abs(offset) == 1 else far_in.at[side],
            send_sem=near_send.at[number],
            recv_sem=near_recv.at[number],
            device_id=(grp, me + offset),
            device_id_type=mesh_id,
        ))
    for number in (0, 3, 1, 2):
        pl.when(there[OFFSETS[number]])(near[number].start)
    for step, other in enumerate(others[1:]):
        pl.semaphore_signal(ready.at[step], inc=1, device_id=(other, me), device_id_type=mesh_id)
    window_grad[...] = jnp.zeros_like(window_grad)
    loads[1].wait()
    prepare_hot(corner, hot)
    loads[7].wait()
    prepare_taps(psf, tap_rows, tap_cols, blur_left, blur_right)
    for copy in loads[2:7]:
        copy.wait()
    for number, offset in enumerate(OFFSETS):
        pl.when(there[-offset])(near[number].wait_recv)
    for step in range(group_count - 1):
        pl.semaphore_wait(ready.at[step], 1)
    join_sides(me, count, region, far_in, sides)
    for n in range(ITEMS):
        warp(n, me, tiles, corner, weight, region, sides, warped)
    for n in range(ITEMS):
        blur(n, coeff, obs, ivar, warped, lifted, blur_left, misfit_parts)
    for n in range(ITEMS):
        back(n, blur_right, misfit_parts, spread, backward)
    for n in range(ITEMS):
        scatter(n, corner, weight, backward, hot, parts, window_grad)
    gather_tiles(me, tiles, window_grad, gradient, far_gradient)

    home = {}
    for offset in (-2, 2, -1, 1, 0):
        number = OFFSETS.index(offset) if offset else 4
        if abs(offset) == 2:
            source, target = far_gradient.at[number // 3], far_arrived.at[grp, number // 3]
        else:
            source, target = gradient.at[offset + 1], arrived.at[grp, offset + 1]
        home[offset] = [
            pltpu.make_async_remote_copy(
                src_ref=source,
                dst_ref=target,
                send_sem=back_send.at[number],
                recv_sem=back_recv.at[number],
                device_id=(others[step], me + offset),
                device_id_type=mesh_id,
            )
            for step in range(0 if offset else 1, group_count)
        ]

        def leave_for(offset=offset):
            for copy in home[offset]:
                copy.start()

        if offset:
            pl.when(there[offset])(leave_for)
        else:
            leave_for()
    arrived[grp, 1] = gradient[1]
    for number, offset in enumerate(OFFSETS):
        pl.when(there[offset])(near[number].wait_send)
    def wait_all(semaphores, offset):
        number = OFFSETS.index(offset) if offset else 4
        first = 0 if offset else 1
        if abs(offset) == 2:
            whole = far_arrived.at[pl.ds(first, group_count - first), number // 3]
        else:
            whole = arrived.at[pl.ds(first, group_count - first), offset + 1]
        pltpu.make_async_copy(whole, whole, semaphores.at[number]).wait()

    wait_all(back_recv, 0)
    for offset in OFFSETS:
        pl.when(there[-offset])(functools.partial(wait_all, back_recv, offset))
    lane = lax.broadcasted_iota(I32, (ROWS, COLS), 1)
    total = jnp.zeros((ROWS, COLS), F32)
    for g in range(group_count):
        total += arrived[g, 1]
        total += jnp.where(there[1], arrived[g, 0], 0.0)
        total += jnp.where(there[-1], arrived[g, 2], 0.0)
        total += jnp.where(there[2] & (lane >= COLS - ROWS), unpack(far_arrived[g, 0], True), 0.0)
        total += jnp.where(there[-2] & (lane < ROWS), unpack(far_arrived[g, 1], False), 0.0)
    out[...] = sky_here[...] - STEP * total
    wait_all(back_send, 0)
    for offset in OFFSETS:
        pl.when(there[offset])(functools.partial(wait_all, back_send, offset))


def per_device(sky, psf_basis, item_tile, warp_corner, warp_weight, psf_coeff, observed, inv_var):
    group_count = lax.axis_size("grp")
    vmem = pl.BlockSpec(memory_space=pltpu.VMEM)
    dma = pltpu.SemaphoreType.DMA
    hbm = pl.BlockSpec(memory_space=pltpu.HBM)
    coeff = psf_coeff.transpose(0, 2, 1, 3)
    return pl.pallas_call(
        kernel,
        out_shape=jax.ShapeDtypeStruct((ROWS, COLS), F32),
        in_specs=[hbm] * 8,
        out_specs=vmem,
        scratch_shapes=[
            pltpu.SMEM(item_tile.shape, I32),
            pltpu.VMEM(psf_basis.shape, BF16),
            pltpu.VMEM(warp_corner.shape, I32),
            pltpu.VMEM(warp_weight.shape, BF16),
            pltpu.VMEM(coeff.shape, BF16),
            pltpu.VMEM(observed.shape, BF16),
            pltpu.VMEM(inv_var.shape, BF16),
            pltpu.VMEM((5, ROWS + 2 * PAD, COLS), F32),
            pltpu.VMEM((2, 8, COLS), F32),
            pltpu.VMEM((2, 8, COLS), F32),
            pltpu.VMEM((group_count, 3, ROWS, COLS), F32),
            pltpu.VMEM((group_count, 2, 8, COLS), F32),
            pltpu.VMEM((3, ROWS + 2 * PAD, COLS), F32),
            pltpu.VMEM((NPSF, COLS, COLS), F32),
            pltpu.VMEM((NPSF, COLS, COLS), F32),
            pltpu.VMEM((NPSF * ROWS, GROUPS_OF_4 * COLS), BF16),
            pltpu.VMEM((GROUPS_OF_4 * COLS, NPSF * ROWS), BF16),
            pltpu.VMEM((ITEMS, 4, EXTENT, 8 * COLS), BF16),
            pltpu.VMEM((ITEMS, ROWS, COLS), F32),
            pltpu.VMEM((ITEMS, DEPTH, 2 * COLS), BF16),
            pltpu.VMEM((ITEMS, NPSF * ROWS, 2 * COLS), BF16),
            pltpu.VMEM((ITEMS, DEPTH, 2 * COLS), F32),
            pltpu.VMEM((ITEMS, ROWS, COLS), F32),
            pltpu.VMEM((ITEMS, 4, 2, ROWS, COLS), F32),
            pltpu.VMEM((ITEMS, 2, ROWS + 8, 2 * COLS), F32),
            pltpu.VMEM((3, ROWS, COLS), F32),
            pltpu.VMEM((2, 8, COLS), F32),
            dma((8,)), dma((4,)), dma((4,)), dma((5,)), dma((5,)),
            pltpu.SemaphoreType.REGULAR((group_count - 1,)),
        ],
        compiler_params=pltpu.CompilerParams(
            collective_id=0, has_side_effects=True, vmem_limit_bytes=int(53.91 * 2**20)
        ),
    )(item_tile, sky, psf_basis, warp_corner, warp_weight, coeff, observed, inv_var)


def solution(mesh):
    return jax.shard_map(
        per_device,
        mesh=mesh,
        in_specs=(
            P(None, "tile"),
            P("grp", None, None, None),
            P(("grp", "tile")),
            P(("grp", "tile"), None, None),
            P(("grp", "tile"), None, None, None),
            P(("grp", "tile"), None, None, None),
            P(("grp", "tile"), None, None),
            P(("grp", "tile"), None, None),
        ),
        out_specs=P(None, "tile"),
        check_vma=False,
    )
```

```python
import functools

import jax
import jax.numpy as jnp
from jax import lax
from jax.experimental import pallas as pl
from jax.experimental.pallas import tpu as pltpu
from jax.sharding import PartitionSpec as P

F32, BF16, I32 = jnp.float32, jnp.bfloat16, jnp.int32
ROWS, COLS, MARGIN, TAPS, NPSF, ITEMS = 32, 128, 24, 41, 5, 3
EXTENT = COLS + 2 * MARGIN
HALF = TAPS // 2
WIDE = ITEMS * COLS
DEPTH = TAPS * ROWS
GROUPS_OF_4 = (TAPS + 3) // 4
PAD = 8
STEP = 0.25
OFFSETS = (-2, -1, 1, 2)
SLOT = {-2: 0, -1: 1, 0: 2, 1: 3, 2: 4}


def split(value):
    high = value.astype(BF16)
    return high, (value - high.astype(F32)).astype(BF16)


def nt_dot(a, b):
    return lax.dot_general(a, b, (((1,), (1,)), ((), ())), preferred_element_type=F32)


def pack(value, right):
    lane_group = lax.broadcasted_iota(I32, (8, COLS), 1) // ROWS
    packed = jnp.zeros((8, COLS), F32)
    for i in range(4):
        turned = pltpu.roll(value[8 * i : 8 * i + 8], (32 * i + (ROWS if right else 0)) % COLS, 1)
        packed = jnp.where(lane_group == i, turned, packed)
    return packed


def unpack(packed, right):
    return jnp.concatenate(
        [pltpu.roll(packed, (-32 * i - (ROWS if right else 0)) % COLS, 1) for i in range(4)], axis=0
    )


def prepare_hot(corner, hot):
    column = lax.broadcasted_iota(I32, (EXTENT, COLS), 0)

    def hot_rows(step, _):
        n, block = step // 4, lax.rem(step, 4)
        at = corner[n, pl.ds(pl.multiple_of(block * 8, 8), 8), :]
        start = at - ((at * 23832) >> 22) * EXTENT
        for u in range(8):
            row = jnp.broadcast_to(start[u : u + 1], (EXTENT, COLS))
            hot[n, block, :, pl.ds(u * COLS, COLS)] = jnp.where(column == row, 1.0, 0.0).astype(BF16)
        return 0

    lax.fori_loop(0, ITEMS * 4, hot_rows, 0)


def prepare_taps(psf, tap_rows, tap_cols, blur_left, blur_right):
    tap_rows[...] = jnp.zeros_like(tap_rows)
    for k in range(NPSF):
        tap_rows[k, pl.ds(0, TAPS), pl.ds(0, TAPS)] = psf[0, k].astype(F32)
    for k in range(NPSF):
        tap_cols[k] = pltpu.roll(tap_rows[k], 4, 0).T
    lane_group = lax.broadcasted_iota(I32, (8, COLS), 1) // ROWS
    for j in range(GROUPS_OF_4):
        whole = []
        for k in range(NPSF):
            for r0 in range(0, ROWS, 8):
                tile = jnp.zeros((8, COLS), F32)
                for part in range(4):
                    row = jnp.broadcast_to(tap_cols[k, pl.ds(4 * j + part, 1), :], (8, COLS))
                    turned = pltpu.roll(row, (r0 + ROWS * part - HALF - 4) % COLS, 1, stride=1, stride_axis=0)
                    tile = turned if part == 0 else jnp.where(lane_group == part, turned, tile)
                whole.append(tile)
        whole = jnp.concatenate(whole, axis=0)
        blur_left[:, pl.ds(j * COLS, COLS)] = whole.astype(BF16)
        blur_right[pl.ds(j * COLS, COLS), :] = whole.T.astype(BF16)


def join_sides(me, count, region, far_in, sides):
    lane = lax.broadcasted_iota(I32, (ROWS, COLS), 1)
    for t in range(3):
        left = unpack(far_in[1], True) if t == 0 else region[t, pl.ds(PAD, ROWS), :]
        right = unpack(far_in[0], False) if t == 2 else region[t + 2, pl.ds(PAD, ROWS), :]
        if t < 2:
            left = jnp.where(me - 2 + t >= 0, left, 0.0)
        if t > 0:
            right = jnp.where(me + t <= count - 1, right, 0.0)
        sides[t, pl.ds(PAD, ROWS), :] = jnp.where(lane >= COLS // 2, left, right)


def warp(n, me, tiles, corner, weight, region, sides, warped):
    t = jnp.clip(tiles[n] - (me - 1), 0, 2)
    for r0 in range(0, ROWS, 8):
        at = corner[n, pl.ds(r0, 8), :]
        q = (at * 23832) >> 22
        p = at - q * EXTENT
        rel = q - (lax.broadcasted_iota(I32, (8, COLS), 0) + r0) + 3
        total = jnp.zeros((8, COLS), F32)
        for dp in range(2):
            index = (p + (dp + COLS - MARGIN)) & (COLS - 1)
            middle = (p + dp >= MARGIN) & (p + dp < MARGIN + COLS)
            upper = jnp.zeros((8, COLS), F32)
            lower = jnp.zeros((8, COLS), F32)
            for o in range(8):
                rows = pl.ds(r0 + (PAD - 3 + o), 8)
                inside = jnp.take_along_axis(region[t + 1, rows, :], index, axis=1)
                beside = jnp.take_along_axis(sides[t, rows, :], index, axis=1)
                found = jnp.where(middle, inside, beside)
                if o < 7:
                    upper = jnp.where(rel == o, found, upper)
                if o > 0:
                    lower = jnp.where(rel == o - 1, found, lower)
            total += weight[n, dp, pl.ds(r0, 8), :].astype(F32) * upper
            total += weight[n, 2 + dp, pl.ds(r0, 8), :].astype(F32) * lower
        warped[n, pl.ds(r0, 8), :] = total


def blur(n, coeff, obs, ivar, warped, lifted, blur_left, misfit_parts):
    lane = lax.broadcasted_iota(I32, (ROWS, COLS), 1)
    for b in range(TAPS):
        source = lane + (b - HALF)
        inside = (source >= 0) & (source < COLS)
        value = warped[n]
        if b != HALF:
            value = jnp.where(inside, pltpu.roll(value, (HALF - b) % COLS, 1), 0.0)
        high, low = split(value)
        lifted[n, pl.ds(b * ROWS, ROWS), pl.ds(0, COLS)] = high
        lifted[n, pl.ds(b * ROWS, ROWS), pl.ds(COLS, COLS)] = low
    both = jnp.dot(blur_left[:, pl.ds(0, DEPTH)], lifted[n], preferred_element_type=F32)
    blurred = both[:, :COLS] + both[:, COLS:]
    predicted = jnp.zeros((ROWS, COLS), F32)
    for k in range(NPSF):
        predicted += coeff[n, k].astype(F32) * blurred[k * ROWS : (k + 1) * ROWS]
    misfit = ivar[n].astype(F32) * (predicted - obs[n].astype(F32))
    for k in range(NPSF):
        high, low = split(coeff[n, k].astype(F32) * misfit)
        misfit_parts[n, pl.ds(k * ROWS, ROWS), pl.ds(0, COLS)] = high
        misfit_parts[n, pl.ds(k * ROWS, ROWS), pl.ds(COLS, COLS)] = low


def back(n, blur_right, misfit_parts, spread, backward):
    lane = lax.broadcasted_iota(I32, (ROWS, COLS), 1)
    spread[n] = jnp.dot(blur_right[pl.ds(0, DEPTH), :], misfit_parts[n], preferred_element_type=F32)
    total = jnp.zeros((ROWS, COLS), F32)
    for b in range(TAPS):
        source = lane - (b - HALF)
        inside = (source >= 0) & (source < COLS)
        value = spread[n, pl.ds(b * ROWS, ROWS), pl.ds(0, COLS)] + spread[n, pl.ds(b * ROWS, ROWS), pl.ds(COLS, COLS)]
        if b != HALF:
            value = jnp.where(inside, pltpu.roll(value, (b - HALF) % COLS, 1), 0.0)
        total += value
    backward[n] = total


def scatter(n, corner, weight, backward, hot, parts, window_grad):
    target = lax.broadcasted_iota(I32, (16, COLS), 0)
    for j in range(4):
        value = weight[n, j].astype(F32) * backward[n]
        high = value.astype(BF16).astype(F32)
        parts[n, j, 0] = high
        parts[n, j, 1] = value - high
    for block in range(4):
        r0 = block * 8
        q = ((corner[n, pl.ds(r0, 8), :] * 23832) >> 22) - (r0 - 4)
        columns = []
        for u in range(8):
            row = jnp.broadcast_to(q[u : u + 1], (16, COLS))
            first, second = target == row, target == row + 1
            stack = []
            for dp in range(2):
                for half in range(2):
                    one_up = jnp.broadcast_to(parts[n, dp, half, pl.ds(r0 + u, 1), :], (16, COLS))
                    one_low = jnp.broadcast_to(parts[n, 2 + dp, half, pl.ds(r0 + u, 1), :], (16, COLS))
                    stack.append(jnp.where(first, one_up, jnp.where(second, one_low, 0.0)).astype(BF16))
            columns.append(jnp.concatenate(stack, axis=0))
        values = jnp.concatenate(columns, axis=1)
        found = nt_dot(values, hot[n, block])
        for dp in range(2):
            part = found[dp * 32 : dp * 32 + 16] + found[dp * 32 + 16 : dp * 32 + 32]
            window_grad[n, dp, pl.ds(r0, 16), pl.ds(0, EXTENT)] += part


def window_parts(me, tiles, window_grad):
    left_lanes = lax.broadcasted_iota(I32, (ROWS, COLS), 1) >= COLS // 2
    found = []
    for n in range(ITEMS):
        whole = pltpu.roll(window_grad[n, 0, pl.ds(4, ROWS), :], COLS - MARGIN, 1)
        whole += pltpu.roll(window_grad[n, 1, pl.ds(4, ROWS), :], COLS - MARGIN + 1, 1)
        beside, inside = whole[:, :COLS], whole[:, COLS:]
        left = jnp.where(left_lanes, beside, 0.0)
        right = jnp.where(left_lanes, 0.0, beside)
        found.append((jnp.clip(tiles[n] - (me - 1), 0, 2), left, inside, right))
    return found


def tile_total(found, slot):
    total = jnp.zeros((ROWS, COLS), F32)
    for n, (t, *three) in enumerate(found):
        for place, part in enumerate(three):
            if 0 <= slot - place <= 2 and (n > 0 or slot - place == 1):
                total += jnp.where(t == slot - place, part, 0.0)
    return total


def kernel(tiles_hbm, sky_hbm, psf_hbm, corner_hbm, weight_hbm, coeff_hbm, obs_hbm, ivar_hbm, out,
           tiles, psf, corner, weight, coeff, obs, ivar,
           region, far_out, far_in, arrived, far_arrived, sides, tap_rows, tap_cols, blur_left, blur_right,
           hot, warped, lifted, misfit_parts, spread, backward, parts, window_grad, gradient, far_gradient,
           load, near_send, near_recv, back_send, back_recv, ready):
    me, grp = lax.axis_index("tile"), lax.axis_index("grp")
    count, group_count = lax.axis_size("tile"), lax.axis_size("grp")
    mesh_id = pl.DeviceIdType.MESH
    there = {offset: (me + offset >= 0) & (me + offset <= count - 1) for offset in OFFSETS}
    others = [lax.rem(grp + step, group_count) for step in range(group_count)]
    barrier = pltpu.get_barrier_semaphore()
    for offset in OFFSETS:
        @pl.when(there[offset])
        def _():
            pl.semaphore_signal(barrier, inc=1, device_id=(grp, me + offset), device_id_type=mesh_id)
    for other in others[1:]:
        pl.semaphore_signal(barrier, inc=1, device_id=(other, me), device_id_type=mesh_id)
    sky_here = region.at[2, pl.ds(PAD, ROWS), :]
    pairs = ((sky_hbm, sky_here), (corner_hbm, corner), (weight_hbm, weight),
             (coeff_hbm, coeff), (obs_hbm, obs), (ivar_hbm, ivar), (tiles_hbm, tiles), (psf_hbm, psf))
    loads = [pltpu.make_async_copy(a, b, load.at[i]) for i, (a, b) in enumerate(pairs)]
    for copy in loads:
        copy.start()
    loads[0].wait()
    far_out[0] = pack(sky_here[...], False)
    far_out[1] = pack(sky_here[...], True)
    neighbours = jnp.minimum(me, 2) + jnp.minimum(count - 1 - me, 2)
    pl.semaphore_wait(barrier, neighbours + group_count - 1)

    near = []
    for number, offset in enumerate(OFFSETS):
        side = 0 if offset < 0 else 1
        near.append(pltpu.make_async_remote_copy(
            src_ref=sky_here if abs(offset) == 1 else far_out.at[side],
            dst_ref=region.at[SLOT[-offset], pl.ds(PAD, ROWS), :] if abs(offset) == 1 else far_in.at[side],
            send_sem=near_send.at[number],
            recv_sem=near_recv.at[number],
            device_id=(grp, me + offset),
            device_id_type=mesh_id,
        ))
    for number in (0, 3, 1, 2):
        pl.when(there[OFFSETS[number]])(near[number].start)
    for step, other in enumerate(others[1:]):
        pl.semaphore_signal(ready.at[step], inc=1, device_id=(other, me), device_id_type=mesh_id)
    window_grad[...] = jnp.zeros_like(window_grad)
    loads[1].wait()
    prepare_hot(corner, hot)
    loads[7].wait()
    prepare_taps(psf, tap_rows, tap_cols, blur_left, blur_right)
    for copy in loads[2:7]:
        copy.wait()
    for number, offset in enumerate(OFFSETS):
        pl.when(there[-offset])(near[number].wait_recv)
    for step in range(group_count - 1):
        pl.semaphore_wait(ready.at[step], 1)
    join_sides(me, count, region, far_in, sides)
    for n in range(ITEMS):
        warp(n, me, tiles, corner, weight, region, sides, warped)
    for n in range(ITEMS):
        blur(n, coeff, obs, ivar, warped, lifted, blur_left, misfit_parts)
    for n in range(ITEMS):
        back(n, blur_right, misfit_parts, spread, backward)
    for n in range(ITEMS):
        scatter(n, corner, weight, backward, hot, parts, window_grad)
    found = window_parts(me, tiles, window_grad)
    far_gradient[0] = pack(tile_total(found, 0), True)
    far_gradient[1] = pack(tile_total(found, 4), False)

    home = {}
    for offset in (-2, 2, -1, 1, 0):
        if offset == -1:
            for slot in range(3):
                gradient[slot] = tile_total(found, slot + 1)
        number = OFFSETS.index(offset) if offset else 4
        if abs(offset) == 2:
            source, target = far_gradient.at[number // 3], far_arrived.at[grp, number // 3]
        else:
            source, target = gradient.at[offset + 1], arrived.at[grp, offset + 1]
        home[offset] = [
            pltpu.make_async_remote_copy(
                src_ref=source,
                dst_ref=target,
                send_sem=back_send.at[number],
                recv_sem=back_recv.at[number],
                device_id=(others[step], me + offset),
                device_id_type=mesh_id,
            )
            for step in range(0 if offset else 1, group_count)
        ]

        def leave_for(offset=offset):
            for copy in home[offset]:
                copy.start()

        if offset:
            pl.when(there[offset])(leave_for)
        else:
            leave_for()
    arrived[grp, 1] = gradient[1]
    for number, offset in enumerate(OFFSETS):
        pl.when(there[offset])(near[number].wait_send)
    def wait_all(semaphores, offset):
        number = OFFSETS.index(offset) if offset else 4
        first = 0 if offset else 1
        if abs(offset) == 2:
            whole = far_arrived.at[pl.ds(first, group_count - first), number // 3]
        else:
            whole = arrived.at[pl.ds(first, group_count - first), offset + 1]
        pltpu.make_async_copy(whole, whole, semaphores.at[number]).wait()

    wait_all(back_recv, 0)
    for offset in OFFSETS:
        pl.when(there[-offset])(functools.partial(wait_all, back_recv, offset))
    lane = lax.broadcasted_iota(I32, (ROWS, COLS), 1)
    total = jnp.zeros((ROWS, COLS), F32)
    for g in range(group_count):
        total += arrived[g, 1]
        total += jnp.where(there[1], arrived[g, 0], 0.0)
        total += jnp.where(there[-1], arrived[g, 2], 0.0)
        total += jnp.where(there[2] & (lane >= COLS - ROWS), unpack(far_arrived[g, 0], True), 0.0)
        total += jnp.where(there[-2] & (lane < ROWS), unpack(far_arrived[g, 1], False), 0.0)
    out[...] = sky_here[...] - STEP * total
    wait_all(back_send, 0)
    for offset in OFFSETS:
        pl.when(there[offset])(functools.partial(wait_all, back_send, offset))


def per_device(sky, psf_basis, item_tile, warp_corner, warp_weight, psf_coeff, observed, inv_var):
    group_count = lax.axis_size("grp")
    vmem = pl.BlockSpec(memory_space=pltpu.VMEM)
    dma = pltpu.SemaphoreType.DMA
    hbm = pl.BlockSpec(memory_space=pltpu.HBM)
    coeff = psf_coeff.transpose(0, 2, 1, 3)
    return pl.pallas_call(
        kernel,
        out_shape=jax.ShapeDtypeStruct((ROWS, COLS), F32),
        in_specs=[hbm] * 8,
        out_specs=vmem,
        scratch_shapes=[
            pltpu.SMEM(item_tile.shape, I32),
            pltpu.VMEM(psf_basis.shape, BF16),
            pltpu.VMEM(warp_corner.shape, I32),
            pltpu.VMEM(warp_weight.shape, BF16),
            pltpu.VMEM(coeff.shape, BF16),
            pltpu.VMEM(observed.shape, BF16),
            pltpu.VMEM(inv_var.shape, BF16),
            pltpu.VMEM((5, ROWS + 2 * PAD, COLS), F32),
            pltpu.VMEM((2, 8, COLS), F32),
            pltpu.VMEM((2, 8, COLS), F32),
            pltpu.VMEM((group_count, 3, ROWS, COLS), F32),
            pltpu.VMEM((group_count, 2, 8, COLS), F32),
            pltpu.VMEM((3, ROWS + 2 * PAD, COLS), F32),
            pltpu.VMEM((NPSF, COLS, COLS), F32),
            pltpu.VMEM((NPSF, COLS, COLS), F32),
            pltpu.VMEM((NPSF * ROWS, GROUPS_OF_4 * COLS), BF16),
            pltpu.VMEM((GROUPS_OF_4 * COLS, NPSF * ROWS), BF16),
            pltpu.VMEM((ITEMS, 4, EXTENT, 8 * COLS), BF16),
            pltpu.VMEM((ITEMS, ROWS, COLS), F32),
            pltpu.VMEM((ITEMS, DEPTH, 2 * COLS), BF16),
            pltpu.VMEM((ITEMS, NPSF * ROWS, 2 * COLS), BF16),
            pltpu.VMEM((ITEMS, DEPTH, 2 * COLS), F32),
            pltpu.VMEM((ITEMS, ROWS, COLS), F32),
            pltpu.VMEM((ITEMS, 4, 2, ROWS, COLS), F32),
            pltpu.VMEM((ITEMS, 2, ROWS + 8, 2 * COLS), F32),
            pltpu.VMEM((3, ROWS, COLS), F32),
            pltpu.VMEM((2, 8, COLS), F32),
            dma((8,)), dma((4,)), dma((4,)), dma((5,)), dma((5,)),
            pltpu.SemaphoreType.REGULAR((group_count - 1,)),
        ],
        compiler_params=pltpu.CompilerParams(
            collective_id=0, has_side_effects=True, vmem_limit_bytes=int(53.91 * 2**20)
        ),
    )(item_tile, sky, psf_basis, warp_corner, warp_weight, coeff, observed, inv_var)


def solution(mesh):
    return jax.shard_map(
        per_device,
        mesh=mesh,
        in_specs=(
            P(None, "tile"),
            P("grp", None, None, None),
            P(("grp", "tile")),
            P(("grp", "tile"), None, None),
            P(("grp", "tile"), None, None, None),
            P(("grp", "tile"), None, None, None),
            P(("grp", "tile"), None, None),
            P(("grp", "tile"), None, None),
        ),
        out_specs=P(None, "tile"),
        check_vma=False,
    )
```

```python
import functools

import jax
import jax.numpy as jnp
from jax import lax
from jax.experimental import pallas as pl
from jax.experimental.pallas import tpu as pltpu
from jax.sharding import PartitionSpec as P

F32, BF16, I32 = jnp.float32, jnp.bfloat16, jnp.int32
ROWS, COLS, MARGIN, TAPS, NPSF, ITEMS = 32, 128, 24, 41, 5, 3
EXTENT = COLS + 2 * MARGIN
HALF = TAPS // 2
WIDE = ITEMS * COLS
DEPTH = TAPS * ROWS
GROUPS_OF_4 = (TAPS + 3) // 4
PAD = 8
STEP = 0.25
OFFSETS = (-2, -1, 1, 2)
SLOT = {-2: 0, -1: 1, 0: 2, 1: 3, 2: 4}


def split(value):
    high = value.astype(BF16)
    return high, (value - high.astype(F32)).astype(BF16)


def nt_dot(a, b):
    return lax.dot_general(a, b, (((1,), (1,)), ((), ())), preferred_element_type=F32)


def pack(value, right):
    lane_group = lax.broadcasted_iota(I32, (8, COLS), 1) // ROWS
    packed = jnp.zeros((8, COLS), F32)
    for i in range(4):
        turned = pltpu.roll(value[8 * i : 8 * i + 8], (32 * i + (ROWS if right else 0)) % COLS, 1)
        packed = jnp.where(lane_group == i, turned, packed)
    return packed


def unpack(packed, right):
    return jnp.concatenate(
        [pltpu.roll(packed, (-32 * i - (ROWS if right else 0)) % COLS, 1) for i in range(4)], axis=0
    )


def prepare_hot(corner, hot):
    column = lax.broadcasted_iota(I32, (EXTENT, COLS), 0)

    def hot_rows(step, _):
        n, block = step // 4, lax.rem(step, 4)
        at = corner[n, pl.ds(pl.multiple_of(block * 8, 8), 8), :]
        start = at - ((at * 23832) >> 22) * EXTENT
        for u in range(8):
            row = jnp.broadcast_to(start[u : u + 1], (EXTENT, COLS))
            hot[n, block, :, pl.ds(u * COLS, COLS)] = jnp.where(column == row, 1.0, 0.0).astype(BF16)
        return 0

    lax.fori_loop(0, ITEMS * 4, hot_rows, 0)


def prepare_taps(psf, tap_rows, tap_cols, blur_left, blur_right):
    tap_rows[...] = jnp.zeros_like(tap_rows)
    for k in range(NPSF):
        tap_rows[k, pl.ds(0, TAPS), pl.ds(0, TAPS)] = psf[0, k].astype(F32)
    for k in range(NPSF):
        tap_cols[k] = pltpu.roll(tap_rows[k], 4, 0).T
    lane_group = lax.broadcasted_iota(I32, (8, COLS), 1) // ROWS
    for j in range(GROUPS_OF_4):
        whole = []
        for k in range(NPSF):
            for r0 in range(0, ROWS, 8):
                tile = jnp.zeros((8, COLS), F32)
                for part in range(4):
                    row = jnp.broadcast_to(tap_cols[k, pl.ds(4 * j + part, 1), :], (8, COLS))
                    turned = pltpu.roll(row, (r0 + ROWS * part - HALF - 4) % COLS, 1, stride=1, stride_axis=0)
                    tile = turned if part == 0 else jnp.where(lane_group == part, turned, tile)
                whole.append(tile)
        whole = jnp.concatenate(whole, axis=0)
        blur_left[:, pl.ds(j * COLS, COLS)] = whole.astype(BF16)
        blur_right[pl.ds(j * COLS, COLS), :] = whole.T.astype(BF16)


def join_sides(me, count, region, far_in, sides):
    lane = lax.broadcasted_iota(I32, (ROWS, COLS), 1)
    for t in range(3):
        left = unpack(far_in[1], True) if t == 0 else region[t, pl.ds(PAD, ROWS), :]
        right = unpack(far_in[0], False) if t == 2 else region[t + 2, pl.ds(PAD, ROWS), :]
        if t < 2:
            left = jnp.where(me - 2 + t >= 0, left, 0.0)
        if t > 0:
            right = jnp.where(me + t <= count - 1, right, 0.0)
        sides[t, pl.ds(PAD, ROWS), :] = jnp.where(lane >= COLS // 2, left, right)


def warp(n, me, tiles, corner, weight, region, sides, warped):
    t = jnp.clip(tiles[n] - (me - 1), 0, 2)
    for r0 in range(0, ROWS, 8):
        at = corner[n, pl.ds(r0, 8), :]
        q = (at * 23832) >> 22
        p = at - q * EXTENT
        rel = q - (lax.broadcasted_iota(I32, (8, COLS), 0) + r0) + 3
        total = jnp.zeros((8, COLS), F32)
        for dp in range(2):
            index = (p + (dp + COLS - MARGIN)) & (COLS - 1)
            middle = (p + dp >= MARGIN) & (p + dp < MARGIN + COLS)
            upper = jnp.zeros((8, COLS), F32)
            lower = jnp.zeros((8, COLS), F32)
            for o in range(8):
                rows = pl.ds(r0 + (PAD - 3 + o), 8)
                inside = jnp.take_along_axis(region[t + 1, rows, :], index, axis=1)
                beside = jnp.take_along_axis(sides[t, rows, :], index, axis=1)
                found = jnp.where(middle, inside, beside)
                if o < 7:
                    upper = jnp.where(rel == o, found, upper)
                if o > 0:
                    lower = jnp.where(rel == o - 1, found, lower)
            total += weight[n, dp, pl.ds(r0, 8), :].astype(F32) * upper
            total += weight[n, 2 + dp, pl.ds(r0, 8), :].astype(F32) * lower
        warped[n, pl.ds(r0, 8), :] = total


def blur(n, coeff, obs, ivar, warped, lifted, blur_left, misfit_parts):
    lane = lax.broadcasted_iota(I32, (ROWS, COLS), 1)
    for b in range(TAPS):
        source = lane + (b - HALF)
        inside = (source >= 0) & (source < COLS)
        value = warped[n]
        if b != HALF:
            value = jnp.where(inside, pltpu.roll(value, (HALF - b) % COLS, 1), 0.0)
        high, low = split(value)
        lifted[n, pl.ds(b * ROWS, ROWS), pl.ds(0, COLS)] = high
        lifted[n, pl.ds(b * ROWS, ROWS), pl.ds(COLS, COLS)] = low
    both = jnp.dot(blur_left[:, pl.ds(0, DEPTH)], lifted[n], preferred_element_type=F32)
    blurred = both[:, :COLS] + both[:, COLS:]
    predicted = jnp.zeros((ROWS, COLS), F32)
    for k in range(NPSF):
        predicted += coeff[n, k].astype(F32) * blurred[k * ROWS : (k + 1) * ROWS]
    misfit = ivar[n].astype(F32) * (predicted - obs[n].astype(F32))
    for k in range(NPSF):
        high, low = split(coeff[n, k].astype(F32) * misfit)
        misfit_parts[n, pl.ds(k * ROWS, ROWS), pl.ds(0, COLS)] = high
        misfit_parts[n, pl.ds(k * ROWS, ROWS), pl.ds(COLS, COLS)] = low


def back(n, blur_right, misfit_parts, spread, backward):
    lane = lax.broadcasted_iota(I32, (ROWS, COLS), 1)
    spread[n] = jnp.dot(blur_right[pl.ds(0, DEPTH), :], misfit_parts[n], preferred_element_type=F32)
    total = jnp.zeros((ROWS, COLS), F32)
    for b in range(TAPS):
        source = lane - (b - HALF)
        inside = (source >= 0) & (source < COLS)
        value = spread[n, pl.ds(b * ROWS, ROWS), pl.ds(0, COLS)] + spread[n, pl.ds(b * ROWS, ROWS), pl.ds(COLS, COLS)]
        if b != HALF:
            value = jnp.where(inside, pltpu.roll(value, (b - HALF) % COLS, 1), 0.0)
        total += value
    backward[n] = total


def scatter(n, corner, weight, backward, hot, parts, window_grad):
    target = lax.broadcasted_iota(I32, (16, COLS), 0)
    for j in range(4):
        value = weight[n, j].astype(F32) * backward[n]
        high = value.astype(BF16).astype(F32)
        parts[n, j, 0] = high
        parts[n, j, 1] = value - high
    for block in range(4):
        r0 = block * 8
        q = ((corner[n, pl.ds(r0, 8), :] * 23832) >> 22) - (r0 - 4)
        columns = []
        for u in range(8):
            row = jnp.broadcast_to(q[u : u + 1], (16, COLS))
            first, second = target == row, target == row + 1
            stack = []
            for dp in range(2):
                for half in range(2):
                    one_up = jnp.broadcast_to(parts[n, dp, half, pl.ds(r0 + u, 1), :], (16, COLS))
                    one_low = jnp.broadcast_to(parts[n, 2 + dp, half, pl.ds(r0 + u, 1), :], (16, COLS))
                    stack.append(jnp.where(first, one_up, jnp.where(second, one_low, 0.0)).astype(BF16))
            columns.append(jnp.concatenate(stack, axis=0))
        values = jnp.concatenate(columns, axis=1)
        found = nt_dot(values, hot[n, block])
        for dp in range(2):
            part = found[dp * 32 : dp * 32 + 16] + found[dp * 32 + 16 : dp * 32 + 32]
            window_grad[n, dp, pl.ds(r0, 16), pl.ds(0, EXTENT)] += part


def window_parts(me, tiles, window_grad):
    left_lanes = lax.broadcasted_iota(I32, (ROWS, COLS), 1) >= COLS // 2
    found = []
    for n in range(ITEMS):
        whole = pltpu.roll(window_grad[n, 0, pl.ds(4, ROWS), :], COLS - MARGIN, 1)
        whole += pltpu.roll(window_grad[n, 1, pl.ds(4, ROWS), :], COLS - MARGIN + 1, 1)
        beside, inside = whole[:, :COLS], whole[:, COLS:]
        left = jnp.where(left_lanes, beside, 0.0)
        right = jnp.where(left_lanes, 0.0, beside)
        found.append((jnp.clip(tiles[n] - (me - 1), 0, 2), left, inside, right))
    return found


def tile_total(found, slot):
    total = jnp.zeros((ROWS, COLS), F32)
    for n, (t, *three) in enumerate(found):
        for place, part in enumerate(three):
            if 0 <= slot - place <= 2 and (n > 0 or slot - place == 1):
                total += jnp.where(t == slot - place, part, 0.0)
    return total


def kernel(tiles_hbm, sky_hbm, psf_hbm, corner_hbm, weight_hbm, coeff_hbm, obs_hbm, ivar_hbm, out,
           tiles, psf, corner, weight, coeff, obs, ivar,
           region, far_out, far_in, arrived, far_arrived, sides, tap_rows, tap_cols, blur_left, blur_right,
           hot, warped, lifted, misfit_parts, spread, backward, parts, window_grad, gradient, far_gradient,
           load, near_send, near_recv, back_send, back_recv, ready):
    me, grp = lax.axis_index("tile"), lax.axis_index("grp")
    count, group_count = lax.axis_size("tile"), lax.axis_size("grp")
    mesh_id = pl.DeviceIdType.MESH
    there = {offset: (me + offset >= 0) & (me + offset <= count - 1) for offset in OFFSETS}
    others = [lax.rem(grp + step, group_count) for step in range(group_count)]
    barrier = pltpu.get_barrier_semaphore()
    for offset in OFFSETS:
        @pl.when(there[offset])
        def _():
            pl.semaphore_signal(barrier, inc=1, device_id=(grp, me + offset), device_id_type=mesh_id)
    for other in others[1:]:
        pl.semaphore_signal(barrier, inc=1, device_id=(other, me), device_id_type=mesh_id)
    sky_here = region.at[2, pl.ds(PAD, ROWS), :]
    pairs = ((sky_hbm, sky_here), (corner_hbm, corner), (weight_hbm, weight),
             (coeff_hbm, coeff), (obs_hbm, obs), (ivar_hbm, ivar), (tiles_hbm, tiles), (psf_hbm, psf))
    loads = [pltpu.make_async_copy(a, b, load.at[i]) for i, (a, b) in enumerate(pairs)]
    for copy in loads:
        copy.start()
    loads[0].wait()
    far_out[0] = pack(sky_here[...], False)
    far_out[1] = pack(sky_here[...], True)
    neighbours = jnp.minimum(me, 2) + jnp.minimum(count - 1 - me, 2)
    pl.semaphore_wait(barrier, neighbours + group_count - 1)

    near = []
    for number, offset in enumerate(OFFSETS):
        side = 0 if offset < 0 else 1
        near.append(pltpu.make_async_remote_copy(
            src_ref=sky_here if abs(offset) == 1 else far_out.at[side],
            dst_ref=region.at[SLOT[-offset], pl.ds(PAD, ROWS), :] if abs(offset) == 1 else far_in.at[side],
            send_sem=near_send.at[number],
            recv_sem=near_recv.at[number],
            device_id=(grp, me + offset),
            device_id_type=mesh_id,
        ))
    for number in (0, 3, 1, 2):
        pl.when(there[OFFSETS[number]])(near[number].start)
    for step, other in enumerate(others[1:]):
        pl.semaphore_signal(ready.at[step], inc=1, device_id=(other, me), device_id_type=mesh_id)
    window_grad[...] = jnp.zeros_like(window_grad)
    loads[1].wait()
    prepare_hot(corner, hot)
    loads[7].wait()
    prepare_taps(psf, tap_rows, tap_cols, blur_left, blur_right)
    for copy in loads[2:7]:
        copy.wait()
    for number, offset in enumerate(OFFSETS):
        pl.when(there[-offset])(near[number].wait_recv)
    for step in range(group_count - 1):
        pl.semaphore_wait(ready.at[step], 1)
    join_sides(me, count, region, far_in, sides)
    for n in range(ITEMS):
        warp(n, me, tiles, corner, weight, region, sides, warped)
    for n in range(ITEMS):
        blur(n, coeff, obs, ivar, warped, lifted, blur_left, misfit_parts)
    for n in range(ITEMS):
        back(n, blur_right, misfit_parts, spread, backward)
    for n in range(ITEMS):
        scatter(n, corner, weight, backward, hot, parts, window_grad)
    found = window_parts(me, tiles, window_grad)
    far_gradient[0] = pack(tile_total(found, 0), True)
    far_gradient[1] = pack(tile_total(found, 4), False)

    home = {}
    for offset in (-2, 2, -1, 1, 0):
        if offset == -1:
            for slot in range(3):
                gradient[slot] = tile_total(found, slot + 1)
        number = OFFSETS.index(offset) if offset else 4
        if abs(offset) == 2:
            source, target = far_gradient.at[number // 3], far_arrived.at[grp, number // 3]
        else:
            source, target = gradient.at[offset + 1], arrived.at[grp, offset + 1]
        home[offset] = [
            pltpu.make_async_remote_copy(
                src_ref=source,
                dst_ref=target,
                send_sem=back_send.at[number],
                recv_sem=back_recv.at[number],
                device_id=(others[step], me + offset),
                device_id_type=mesh_id,
            )
            for step in range(0 if offset else 1, group_count)
        ]

        def leave_for(offset=offset):
            for copy in home[offset]:
                copy.start()

        if offset:
            pl.when(there[offset])(leave_for)
        else:
            leave_for()
    arrived[grp, 1] = gradient[1]
    for number, offset in enumerate(OFFSETS):
        pl.when(there[offset])(near[number].wait_send)
    def wait_all(semaphores, offset):
        number = OFFSETS.index(offset) if offset else 4
        first = 0 if offset else 1
        if abs(offset) == 2:
            whole = far_arrived.at[pl.ds(first, group_count - first), number // 3]
        else:
            whole = arrived.at[pl.ds(first, group_count - first), offset + 1]
        pltpu.make_async_copy(whole, whole, semaphores.at[number]).wait()

    wait_all(back_recv, 0)
    for offset in OFFSETS:
        pl.when(there[-offset])(functools.partial(wait_all, back_recv, offset))
    lane = lax.broadcasted_iota(I32, (ROWS, COLS), 1)
    total = jnp.zeros((ROWS, COLS), F32)
    for g in range(group_count):
        total += arrived[g, 1]
        total += jnp.where(there[1], arrived[g, 0], 0.0)
        total += jnp.where(there[-1], arrived[g, 2], 0.0)
        total += jnp.where(there[2] & (lane >= COLS - ROWS), unpack(far_arrived[g, 0], True), 0.0)
        total += jnp.where(there[-2] & (lane < ROWS), unpack(far_arrived[g, 1], False), 0.0)
    out[...] = sky_here[...] - STEP * total
    wait_all(back_send, 0)
    for offset in OFFSETS:
        pl.when(there[offset])(functools.partial(wait_all, back_send, offset))


def per_device(sky, psf_basis, item_tile, warp_corner, warp_weight, psf_coeff, observed, inv_var):
    group_count = lax.axis_size("grp")
    vmem = pl.BlockSpec(memory_space=pltpu.VMEM)
    dma = pltpu.SemaphoreType.DMA
    hbm = pl.BlockSpec(memory_space=pltpu.HBM)
    coeff = psf_coeff.transpose(0, 2, 1, 3)
    return pl.pallas_call(
        kernel,
        out_shape=jax.ShapeDtypeStruct((ROWS, COLS), F32),
        in_specs=[hbm] * 8,
        out_specs=vmem,
        scratch_shapes=[
            pltpu.SMEM(item_tile.shape, I32),
            pltpu.VMEM(psf_basis.shape, BF16),
            pltpu.VMEM(warp_corner.shape, I32),
            pltpu.VMEM(warp_weight.shape, BF16),
            pltpu.VMEM(coeff.shape, BF16),
            pltpu.VMEM(observed.shape, BF16),
            pltpu.VMEM(inv_var.shape, BF16),
            pltpu.VMEM((5, ROWS + 2 * PAD, COLS), F32),
            pltpu.VMEM((2, 8, COLS), F32),
            pltpu.VMEM((2, 8, COLS), F32),
            pltpu.VMEM((group_count, 3, ROWS, COLS), F32),
            pltpu.VMEM((group_count, 2, 8, COLS), F32),
            pltpu.VMEM((3, ROWS + 2 * PAD, COLS), F32),
            pltpu.VMEM((NPSF, COLS, COLS), F32),
            pltpu.VMEM((NPSF, COLS, COLS), F32),
            pltpu.VMEM((NPSF * ROWS, GROUPS_OF_4 * COLS), BF16),
            pltpu.VMEM((GROUPS_OF_4 * COLS, NPSF * ROWS), BF16),
            pltpu.VMEM((ITEMS, 4, EXTENT, 8 * COLS), BF16),
            pltpu.VMEM((ITEMS, ROWS, COLS), F32),
            pltpu.VMEM((ITEMS, DEPTH, 2 * COLS), BF16),
            pltpu.VMEM((ITEMS, NPSF * ROWS, 2 * COLS), BF16),
            pltpu.VMEM((ITEMS, DEPTH, 2 * COLS), F32),
            pltpu.VMEM((ITEMS, ROWS, COLS), F32),
            pltpu.VMEM((ITEMS, 4, 2, ROWS, COLS), F32),
            pltpu.VMEM((ITEMS, 2, ROWS + 8, 2 * COLS), F32),
            pltpu.VMEM((3, ROWS, COLS), F32),
            pltpu.VMEM((2, 8, COLS), F32),
            dma((8,)), dma((4,)), dma((4,)), dma((5,)), dma((5,)),
            pltpu.SemaphoreType.REGULAR((group_count - 1,)),
        ],
        compiler_params=pltpu.CompilerParams(
            collective_id=0, has_side_effects=True, vmem_limit_bytes=62 * 2**20
        ),
    )(item_tile, sky, psf_basis, warp_corner, warp_weight, coeff, observed, inv_var)


def solution(mesh):
    return jax.shard_map(
        per_device,
        mesh=mesh,
        in_specs=(
            P(None, "tile"),
            P("grp", None, None, None),
            P(("grp", "tile")),
            P(("grp", "tile"), None, None),
            P(("grp", "tile"), None, None, None),
            P(("grp", "tile"), None, None, None),
            P(("grp", "tile"), None, None),
            P(("grp", "tile"), None, None),
        ),
        out_specs=P(None, "tile"),
        check_vma=False,
    )
```

```python
import functools

import jax
import jax.numpy as jnp
from jax import lax
from jax.experimental import pallas as pl
from jax.experimental.pallas import tpu as pltpu
from jax.sharding import PartitionSpec as P

F32, BF16, I32 = jnp.float32, jnp.bfloat16, jnp.int32
ROWS, COLS, MARGIN, TAPS, NPSF, ITEMS = 32, 128, 24, 41, 5, 3
EXTENT = COLS + 2 * MARGIN
HALF = TAPS // 2
WIDE = ITEMS * COLS
DEPTH = TAPS * ROWS
GROUPS_OF_4 = (TAPS + 3) // 4
PAD = 8
STEP = 0.25
OFFSETS = (-2, -1, 1, 2)
SLOT = {-2: 0, -1: 1, 0: 2, 1: 3, 2: 4}


def split(value):
    high = value.astype(BF16)
    return high, (value - high.astype(F32)).astype(BF16)


def nt_dot(a, b):
    return lax.dot_general(a, b, (((1,), (1,)), ((), ())), preferred_element_type=F32)


def pack(value, right):
    lane_group = lax.broadcasted_iota(I32, (8, COLS), 1) // ROWS
    packed = jnp.zeros((8, COLS), F32)
    for i in range(4):
        turned = pltpu.roll(value[8 * i : 8 * i + 8], (32 * i + (ROWS if right else 0)) % COLS, 1)
        packed = jnp.where(lane_group == i, turned, packed)
    return packed


def unpack(packed, right):
    return jnp.concatenate(
        [pltpu.roll(packed, (-32 * i - (ROWS if right else 0)) % COLS, 1) for i in range(4)], axis=0
    )


def prepare_hot(corner, hot):
    column = lax.broadcasted_iota(I32, (EXTENT, COLS), 0)

    def hot_rows(step, _):
        n, block = step // 4, lax.rem(step, 4)
        at = corner[n, pl.ds(pl.multiple_of(block * 8, 8), 8), :]
        start = at - ((at * 23832) >> 22) * EXTENT
        for u in range(8):
            row = jnp.broadcast_to(start[u : u + 1], (EXTENT, COLS))
            hot[n, block, :, pl.ds(u * COLS, COLS)] = jnp.where(column == row, 1.0, 0.0).astype(BF16)
        return 0

    lax.fori_loop(0, ITEMS * 4, hot_rows, 0)


def prepare_taps(psf, tap_rows, tap_cols, blur_left, blur_right):
    tap_rows[...] = jnp.zeros_like(tap_rows)
    for k in range(NPSF):
        tap_rows[k, pl.ds(0, TAPS), pl.ds(0, TAPS)] = psf[0, k].astype(F32)
    for k in range(NPSF):
        tap_cols[k] = pltpu.roll(tap_rows[k], 4, 0).T
    lane_group = lax.broadcasted_iota(I32, (8, COLS), 1) // ROWS
    for j in range(GROUPS_OF_4):
        whole = []
        for k in range(NPSF):
            for r0 in range(0, ROWS, 8):
                tile = jnp.zeros((8, COLS), F32)
                for part in range(4):
                    row = jnp.broadcast_to(tap_cols[k, pl.ds(4 * j + part, 1), :], (8, COLS))
                    turned = pltpu.roll(row, (r0 + ROWS * part - HALF - 4) % COLS, 1, stride=1, stride_axis=0)
                    tile = turned if part == 0 else jnp.where(lane_group == part, turned, tile)
                whole.append(tile)
        whole = jnp.concatenate(whole, axis=0)
        blur_left[:, pl.ds(j * COLS, COLS)] = whole.astype(BF16)
        blur_right[pl.ds(j * COLS, COLS), :] = whole.T.astype(BF16)


def join_sides(me, count, region, far_in, sides):
    lane = lax.broadcasted_iota(I32, (ROWS, COLS), 1)
    for t in range(3):
        left = unpack(far_in[1], True) if t == 0 else region[t, pl.ds(PAD, ROWS), :]
        right = unpack(far_in[0], False) if t == 2 else region[t + 2, pl.ds(PAD, ROWS), :]
        if t < 2:
            left = jnp.where(me - 2 + t >= 0, left, 0.0)
        if t > 0:
            right = jnp.where(me + t <= count - 1, right, 0.0)
        sides[t, pl.ds(PAD, ROWS), :] = jnp.where(lane >= COLS // 2, left, right)


def warp(n, me, tiles, corner, weight, region, sides, warped):
    t = jnp.clip(tiles[n] - (me - 1), 0, 2)
    for r0 in range(0, ROWS, 8):
        at = corner[n, pl.ds(r0, 8), :]
        q = (at * 23832) >> 22
        p = at - q * EXTENT
        rel = q - (lax.broadcasted_iota(I32, (8, COLS), 0) + r0) + 3
        total = jnp.zeros((8, COLS), F32)
        for dp in range(2):
            index = (p + (dp + COLS - MARGIN)) & (COLS - 1)
            middle = (p + dp >= MARGIN) & (p + dp < MARGIN + COLS)
            upper = jnp.zeros((8, COLS), F32)
            lower = jnp.zeros((8, COLS), F32)
            for o in range(8):
                rows = pl.ds(r0 + (PAD - 3 + o), 8)
                inside = jnp.take_along_axis(region[t + 1, rows, :], index, axis=1)
                beside = jnp.take_along_axis(sides[t, rows, :], index, axis=1)
                found = jnp.where(middle, inside, beside)
                if o < 7:
                    upper = jnp.where(rel == o, found, upper)
                if o > 0:
                    lower = jnp.where(rel == o - 1, found, lower)
            total += weight[n, dp, pl.ds(r0, 8), :].astype(F32) * upper
            total += weight[n, 2 + dp, pl.ds(r0, 8), :].astype(F32) * lower
        warped[n, pl.ds(r0, 8), :] = total


def blur(n, coeff, obs, ivar, warped, lifted, blur_left, misfit_parts):
    lane = lax.broadcasted_iota(I32, (ROWS, COLS), 1)
    for b in range(TAPS):
        source = lane + (b - HALF)
        inside = (source >= 0) & (source < COLS)
        value = warped[n]
        if b != HALF:
            value = jnp.where(inside, pltpu.roll(value, (HALF - b) % COLS, 1), 0.0)
        high, low = split(value)
        lifted[n, pl.ds(b * ROWS, ROWS), pl.ds(0, COLS)] = high
        lifted[n, pl.ds(b * ROWS, ROWS), pl.ds(COLS, COLS)] = low
    both = jnp.dot(blur_left[:, pl.ds(0, DEPTH)], lifted[n], preferred_element_type=F32)
    blurred = both[:, :COLS] + both[:, COLS:]
    predicted = jnp.zeros((ROWS, COLS), F32)
    for k in range(NPSF):
        predicted += coeff[n, k].astype(F32) * blurred[k * ROWS : (k + 1) * ROWS]
    misfit = ivar[n].astype(F32) * (predicted - obs[n].astype(F32))
    for k in range(NPSF):
        high, low = split(coeff[n, k].astype(F32) * misfit)
        misfit_parts[n, pl.ds(k * ROWS, ROWS), pl.ds(0, COLS)] = high
        misfit_parts[n, pl.ds(k * ROWS, ROWS), pl.ds(COLS, COLS)] = low


def back(n, blur_right, misfit_parts, spread, backward):
    lane = lax.broadcasted_iota(I32, (ROWS, COLS), 1)
    spread[n] = jnp.dot(blur_right[pl.ds(0, DEPTH), :], misfit_parts[n], preferred_element_type=F32)
    total = jnp.zeros((ROWS, COLS), F32)
    for b in range(TAPS):
        source = lane - (b - HALF)
        inside = (source >= 0) & (source < COLS)
        value = spread[n, pl.ds(b * ROWS, ROWS), pl.ds(0, COLS)] + spread[n, pl.ds(b * ROWS, ROWS), pl.ds(COLS, COLS)]
        if b != HALF:
            value = jnp.where(inside, pltpu.roll(value, (b - HALF) % COLS, 1), 0.0)
        total += value
    backward[n] = total


def scatter(n, corner, weight, backward, hot, parts, window_grad):
    target = lax.broadcasted_iota(I32, (16, COLS), 0)
    for j in range(4):
        value = weight[n, j].astype(F32) * backward[n]
        high = value.astype(BF16).astype(F32)
        parts[n, j, 0] = high
        parts[n, j, 1] = value - high
    for block in range(4):
        r0 = block * 8
        q = ((corner[n, pl.ds(r0, 8), :] * 23832) >> 22) - (r0 - 4)
        columns = []
        for u in range(8):
            row = jnp.broadcast_to(q[u : u + 1], (16, COLS))
            first, second = target == row, target == row + 1
            stack = []
            for dp in range(2):
                for half in range(2):
                    one_up = jnp.broadcast_to(parts[n, dp, half, pl.ds(r0 + u, 1), :], (16, COLS))
                    one_low = jnp.broadcast_to(parts[n, 2 + dp, half, pl.ds(r0 + u, 1), :], (16, COLS))
                    stack.append(jnp.where(first, one_up, jnp.where(second, one_low, 0.0)).astype(BF16))
            columns.append(jnp.concatenate(stack, axis=0))
        values = jnp.concatenate(columns, axis=1)
        found = nt_dot(values, hot[n, block])
        for dp in range(2):
            part = found[dp * 32 : dp * 32 + 16] + found[dp * 32 + 16 : dp * 32 + 32]
            window_grad[n, dp, pl.ds(r0, 16), pl.ds(0, EXTENT)] += part


def window_parts(me, tiles, window_grad):
    left_lanes = lax.broadcasted_iota(I32, (ROWS, COLS), 1) >= COLS // 2
    found = []
    for n in range(ITEMS):
        whole = pltpu.roll(window_grad[n, 0, pl.ds(4, ROWS), :], COLS - MARGIN, 1)
        whole += pltpu.roll(window_grad[n, 1, pl.ds(4, ROWS), :], COLS - MARGIN + 1, 1)
        beside, inside = whole[:, :COLS], whole[:, COLS:]
        left = jnp.where(left_lanes, beside, 0.0)
        right = jnp.where(left_lanes, 0.0, beside)
        found.append((jnp.clip(tiles[n] - (me - 1), 0, 2), left, inside, right))
    return found


def tile_total(found, slot):
    total = jnp.zeros((ROWS, COLS), F32)
    for n, (t, *three) in enumerate(found):
        for place, part in enumerate(three):
            if 0 <= slot - place <= 2 and (n > 0 or slot - place == 1):
                total += jnp.where(t == slot - place, part, 0.0)
    return total


def kernel(tiles_hbm, sky_hbm, psf_hbm, corner_hbm, weight_hbm, coeff_hbm, obs_hbm, ivar_hbm, out,
           tiles, psf, corner, weight, coeff, obs, ivar,
           region, far_out, far_in, arrived, far_arrived, sides, tap_rows, tap_cols, blur_left, blur_right,
           hot, warped, lifted, misfit_parts, spread, backward, parts, window_grad, gradient, far_gradient,
           load, near_send, near_recv, back_send, back_recv, ready):
    me, grp = lax.axis_index("tile"), lax.axis_index("grp")
    count, group_count = lax.axis_size("tile"), lax.axis_size("grp")
    mesh_id = pl.DeviceIdType.MESH
    there = {offset: (me + offset >= 0) & (me + offset <= count - 1) for offset in OFFSETS}
    others = [lax.rem(grp + step, group_count) for step in range(group_count)]
    barrier = pltpu.get_barrier_semaphore()
    for offset in OFFSETS:
        @pl.when(there[offset])
        def _():
            pl.semaphore_signal(barrier, inc=1, device_id=(grp, me + offset), device_id_type=mesh_id)
    for other in others[1:]:
        pl.semaphore_signal(barrier, inc=1, device_id=(other, me), device_id_type=mesh_id)
    sky_here = region.at[2, pl.ds(PAD, ROWS), :]
    pairs = ((sky_hbm, sky_here), (corner_hbm, corner), (weight_hbm, weight),
             (coeff_hbm, coeff), (obs_hbm, obs), (ivar_hbm, ivar), (tiles_hbm, tiles), (psf_hbm, psf))
    loads = [pltpu.make_async_copy(a, b, load.at[i]) for i, (a, b) in enumerate(pairs)]
    for copy in loads:
        copy.start()
    loads[0].wait()
    far_out[0] = pack(sky_here[...], False)
    far_out[1] = pack(sky_here[...], True)
    neighbours = jnp.minimum(me, 2) + jnp.minimum(count - 1 - me, 2)
    pl.semaphore_wait(barrier, neighbours + group_count - 1)

    near = []
    for number, offset in enumerate(OFFSETS):
        side = 0 if offset < 0 else 1
        near.append(pltpu.make_async_remote_copy(
            src_ref=sky_here if abs(offset) == 1 else far_out.at[side],
            dst_ref=region.at[SLOT[-offset], pl.ds(PAD, ROWS), :] if abs(offset) == 1 else far_in.at[side],
            send_sem=near_send.at[number],
            recv_sem=near_recv.at[number],
            device_id=(grp, me + offset),
            device_id_type=mesh_id,
        ))
    for number in (0, 3, 1, 2):
        pl.when(there[OFFSETS[number]])(near[number].start)
    for step, other in enumerate(others[1:]):
        pl.semaphore_signal(ready.at[step], inc=1, device_id=(other, me), device_id_type=mesh_id)
    window_grad[...] = jnp.zeros_like(window_grad)
    loads[1].wait()
    prepare_hot(corner, hot)
    loads[7].wait()
    prepare_taps(psf, tap_rows, tap_cols, blur_left, blur_right)
    for copy in loads[2:7]:
        copy.wait()
    for number, offset in enumerate(OFFSETS):
        pl.when(there[-offset])(near[number].wait_recv)
    for step in range(group_count - 1):
        pl.semaphore_wait(ready.at[step], 1)
    join_sides(me, count, region, far_in, sides)
    for n in range(ITEMS):
        warp(n, me, tiles, corner, weight, region, sides, warped)
    for n in range(ITEMS):
        blur(n, coeff, obs, ivar, warped, lifted, blur_left, misfit_parts)
    for n in range(ITEMS):
        back(n, blur_right, misfit_parts, spread, backward)
    for n in range(ITEMS):
        scatter(n, corner, weight, backward, hot, parts, window_grad)
    found = window_parts(me, tiles, window_grad)
    far_gradient[0] = pack(tile_total(found, 0), True)
    far_gradient[1] = pack(tile_total(found, 4), False)

    home = {}
    for offset in (-2, 2, -1, 1, 0):
        if offset == -1:
            for slot in range(3):
                gradient[slot] = tile_total(found, slot + 1)
        number = OFFSETS.index(offset) if offset else 4
        if abs(offset) == 2:
            source, target = far_gradient.at[number // 3], far_arrived.at[grp, number // 3]
        else:
            source, target = gradient.at[offset + 1], arrived.at[grp, offset + 1]
        home[offset] = [
            pltpu.make_async_remote_copy(
                src_ref=source,
                dst_ref=target,
                send_sem=back_send.at[number],
                recv_sem=back_recv.at[number],
                device_id=(others[step], me + offset),
                device_id_type=mesh_id,
            )
            for step in (*range(1, group_count), *((0,) if offset else ()))
        ]

        def leave_for(offset=offset):
            for copy in home[offset]:
                copy.start()

        if offset:
            pl.when(there[offset])(leave_for)
        else:
            leave_for()
    arrived[grp, 1] = gradient[1]
    for number, offset in enumerate(OFFSETS):
        pl.when(there[offset])(near[number].wait_send)
    def wait_all(semaphores, offset):
        number = OFFSETS.index(offset) if offset else 4
        first = 0 if offset else 1
        if abs(offset) == 2:
            whole = far_arrived.at[pl.ds(first, group_count - first), number // 3]
        else:
            whole = arrived.at[pl.ds(first, group_count - first), offset + 1]
        pltpu.make_async_copy(whole, whole, semaphores.at[number]).wait()

    wait_all(back_recv, 0)
    for offset in OFFSETS:
        pl.when(there[-offset])(functools.partial(wait_all, back_recv, offset))
    lane = lax.broadcasted_iota(I32, (ROWS, COLS), 1)
    total = jnp.zeros((ROWS, COLS), F32)
    for g in range(group_count):
        total += arrived[g, 1]
        total += jnp.where(there[1], arrived[g, 0], 0.0)
        total += jnp.where(there[-1], arrived[g, 2], 0.0)
        total += jnp.where(there[2] & (lane >= COLS - ROWS), unpack(far_arrived[g, 0], True), 0.0)
        total += jnp.where(there[-2] & (lane < ROWS), unpack(far_arrived[g, 1], False), 0.0)
    out[...] = sky_here[...] - STEP * total
    wait_all(back_send, 0)
    for offset in OFFSETS:
        pl.when(there[offset])(functools.partial(wait_all, back_send, offset))


def per_device(sky, psf_basis, item_tile, warp_corner, warp_weight, psf_coeff, observed, inv_var):
    group_count = lax.axis_size("grp")
    vmem = pl.BlockSpec(memory_space=pltpu.VMEM)
    dma = pltpu.SemaphoreType.DMA
    hbm = pl.BlockSpec(memory_space=pltpu.HBM)
    coeff = psf_coeff.transpose(0, 2, 1, 3)
    return pl.pallas_call(
        kernel,
        out_shape=jax.ShapeDtypeStruct((ROWS, COLS), F32),
        in_specs=[hbm] * 8,
        out_specs=vmem,
        scratch_shapes=[
            pltpu.SMEM(item_tile.shape, I32),
            pltpu.VMEM(psf_basis.shape, BF16),
            pltpu.VMEM(warp_corner.shape, I32),
            pltpu.VMEM(warp_weight.shape, BF16),
            pltpu.VMEM(coeff.shape, BF16),
            pltpu.VMEM(observed.shape, BF16),
            pltpu.VMEM(inv_var.shape, BF16),
            pltpu.VMEM((5, ROWS + 2 * PAD, COLS), F32),
            pltpu.VMEM((2, 8, COLS), F32),
            pltpu.VMEM((2, 8, COLS), F32),
            pltpu.VMEM((group_count, 3, ROWS, COLS), F32),
            pltpu.VMEM((group_count, 2, 8, COLS), F32),
            pltpu.VMEM((3, ROWS + 2 * PAD, COLS), F32),
            pltpu.VMEM((NPSF, COLS, COLS), F32),
            pltpu.VMEM((NPSF, COLS, COLS), F32),
            pltpu.VMEM((NPSF * ROWS, GROUPS_OF_4 * COLS), BF16),
            pltpu.VMEM((GROUPS_OF_4 * COLS, NPSF * ROWS), BF16),
            pltpu.VMEM((ITEMS, 4, EXTENT, 8 * COLS), BF16),
            pltpu.VMEM((ITEMS, ROWS, COLS), F32),
            pltpu.VMEM((ITEMS, DEPTH, 2 * COLS), BF16),
            pltpu.VMEM((ITEMS, NPSF * ROWS, 2 * COLS), BF16),
            pltpu.VMEM((ITEMS, DEPTH, 2 * COLS), F32),
            pltpu.VMEM((ITEMS, ROWS, COLS), F32),
            pltpu.VMEM((ITEMS, 4, 2, ROWS, COLS), F32),
            pltpu.VMEM((ITEMS, 2, ROWS + 8, 2 * COLS), F32),
            pltpu.VMEM((3, ROWS, COLS), F32),
            pltpu.VMEM((2, 8, COLS), F32),
            dma((8,)), dma((4,)), dma((4,)), dma((5,)), dma((5,)),
            pltpu.SemaphoreType.REGULAR((group_count - 1,)),
        ],
        compiler_params=pltpu.CompilerParams(
            collective_id=0, has_side_effects=True, vmem_limit_bytes=int(53.91 * 2**20)
        ),
    )(item_tile, sky, psf_basis, warp_corner, warp_weight, coeff, observed, inv_var)


def solution(mesh):
    return jax.shard_map(
        per_device,
        mesh=mesh,
        in_specs=(
            P(None, "tile"),
            P("grp", None, None, None),
            P(("grp", "tile")),
            P(("grp", "tile"), None, None),
            P(("grp", "tile"), None, None, None),
            P(("grp", "tile"), None, None, None),
            P(("grp", "tile"), None, None),
            P(("grp", "tile"), None, None),
        ),
        out_specs=P(None, "tile"),
        check_vma=False,
    )
```
